128 devices in a mesh: tables: 16 (over y, x), replica: 8 (over z, core).
Axes of the slice: x: 4, y: 4, z: 4, core: 2. Of those that a mesh axis runs over, the one named last changes fastest.
Arguments:
- core_first: bfloat16 [16, 512, 512], P('tables'), may hold values from -6 to 6
- core_middle: bfloat16 [16, 80, 64, 128], P('tables'), may hold values from -0.75 to 0.75
- core_last: bfloat16 [16, 512, 512], P('tables'), may hold values from -0.75 to 0.75
- idx_first: int32 [8, 16, 320, 16, 2], P('replica', 'tables'), may hold values from 0 to 511
- idx_middle: int32 [8, 16, 320, 16, 2], P('replica', 'tables'), may hold values from 0 to 79
- idx_last: int32 [8, 16, 320, 16, 2], P('replica', 'tables'), may hold values from 0 to 511
- bag_lengths: int32 [8, 16, 320, 16], P('replica', 'tables'), may hold values from 1 to 2
- cross_down: bfloat16 [2, 2048, 256], replicated, may hold values from -0.0625 to 0.0625
- cross_up: bfloat16 [2, 256, 2048], replicated, may hold values from -0.1875 to 0.1875
- cross_bias: bfloat16 [2, 2048], replicated, may hold values from -3 to 3
- top_weight: bfloat16 [2048, 4096], P(None, 'tables'), may hold values from -0.125 to 0.125
- top_bias: bfloat16 [4096], replicated, may hold values from -3 to 3
- out_weight: bfloat16 [4096], replicated, may hold values from -0.09375 to 0.09375
- prior: float32 [8, 16, 320], P('replica', 'tables'), may hold values from -4.5 to 4.5
Outputs:
- logits: float32 [8, 16, 320], P('replica', 'tables')
- click_share: float32 [8, 16, 320], P('replica', 'tables')
The draws below stay inside these ranges and needn't reach their ends.
All inputs are finite; a program needn't handle non-finite values.
Results may differ from the reference program's by a relative error of at most 0.0035.
Values may be sent and summed in bfloat16 or wider, within the bound.
A program may use at most 128 MiB of HBM per device.

```python
import math
import jax
import jax.numpy as jnp
import numpy as np
from jax import lax

D1 = 8
D2 = 2
D3 = 8
RANK = 64
R1 = 512
R2 = 80
R3 = 512
BAG = 2
LAYERS = 2
RANKC = 256
HID = 4096
Q_DEV = 320
TABLES = 16
FEAT = 2048
REPS = 8
SHARDS = 16


def draw_prior(key, part):
    position = (jnp.arange(REPS)[:, None, None] * Q_DEV + jnp.arange(Q_DEV)[None, None, :]).astype(jnp.float32) / (REPS * Q_DEV)
    position = jnp.broadcast_to(position, (REPS, SHARDS, Q_DEV))
    noise = jax.random.uniform(key, (REPS, SHARDS, Q_DEV), jnp.float32, -0.5, 0.5)
    return 3.0 - 6.0 * position + noise


def touch_ends(result, stream_key, least, largest):
    index_at = [jax.random.randint(jax.random.fold_in(stream_key, axis), (), 0, length) for axis, length in enumerate(result.shape)]
    widest = result.shape.index(max(result.shape))
    beside = index_at[:widest] + [(index_at[widest] + 1) % result.shape[widest]] + index_at[widest + 1:]
    return result.at[tuple(index_at)].set(least).at[tuple(beside)].set(largest)


def levels(own_key, dims, cuts, smallest, high):
    gain = 1.0
    for dim, parts in cuts:
        steps = jax.random.uniform(jax.random.fold_in(jax.random.fold_in(own_key, 6), dim), (parts,), jnp.float32, smallest / len(cuts), high / len(cuts))
        gain = gain * jnp.repeat(jnp.exp(steps), dims[dim] // parts).reshape((-1,) + (1,) * (len(dims) - 1 - dim))
    return gain


def cumulative_ranks(count, slope):
    loads = [(1 << 20) // math.isqrt(grade ** slope) + 1 for grade in range(1, count + 1)]
    spread = 1 + sum(loads) // (1 << 30)
    return np.cumsum(np.array([max(1, weight // spread) for weight in loads]))


def ranked_ids(rng, shape, number_of, slope):
    grid = cumulative_ranks(number_of, slope)
    pick = jax.random.randint(jax.random.fold_in(rng, 1), shape, 0, int(grid[number_of - 1]))
    standing = jnp.searchsorted(jnp.asarray(grid, jnp.int32), pick, side="right")
    return jax.random.permutation(jax.random.fold_in(rng, 2), number_of)[standing].astype(jnp.int32)


def normal_values(rng, dims, scale, limit, cuts=(), kind=jnp.bfloat16):
    gain = levels(rng, dims, cuts, -0.22, 0.18) if cuts else 1.0
    entries = jax.random.normal(rng, dims, jnp.float32) * scale * gain
    return jnp.minimum(jnp.maximum(entries, -limit), limit).astype(kind)


def setup_inputs(seed: int = 0) -> dict:
    key_of = jax.random.split(jax.random.key(seed), 15)
    return {
        "core_first": normal_values(key_of[0], (TABLES, R1, D1 * RANK), 1.0, 6.0, ((0, 16),)),
        "core_middle": normal_values(key_of[1], (TABLES, R2, RANK, D2 * RANK), RANK ** -0.5, 0.75, ((0, 16),)),
        "core_last": normal_values(key_of[2], (TABLES, R3, RANK * D3), RANK ** -0.5, 0.75, ((0, 16),)),
        "idx_first": touch_ends(ranked_ids(key_of[3], (REPS, SHARDS, Q_DEV, TABLES, BAG), R1, 2), jax.random.fold_in(key_of[3], 3), 0, R1 - 1).astype(jnp.int32),
        "idx_middle": touch_ends(jax.random.randint(key_of[4], (REPS, SHARDS, Q_DEV, TABLES, BAG), 0, R2), jax.random.fold_in(key_of[4], 1), 0, R2 - 1).astype(jnp.int32),
        "idx_last": touch_ends(jax.random.randint(key_of[5], (REPS, SHARDS, Q_DEV, TABLES, BAG), 0, R3), jax.random.fold_in(key_of[5], 1), 0, R3 - 1).astype(jnp.int32),
        "bag_lengths": touch_ends(jax.random.randint(key_of[6], (REPS, SHARDS, Q_DEV, TABLES), 1, BAG + 1), jax.random.fold_in(key_of[6], 1), 1, BAG).astype(jnp.int32),
        "cross_down": normal_values(key_of[7], (LAYERS, FEAT, RANKC), (4 * FEAT) ** -0.5, 0.0625),
        "cross_up": normal_values(key_of[8], (LAYERS, RANKC, FEAT), (4 * RANKC) ** -0.5, 0.1875),
        "cross_bias": normal_values(key_of[9], (LAYERS, FEAT), 0.5, 3.0),
        "top_weight": normal_values(key_of[10], (FEAT, HID), FEAT ** -0.5, 0.125, ((1, 16),)),
        "top_bias": normal_values(key_of[11], (HID,), 0.5, 3.0),
        "out_weight": normal_values(key_of[12], (HID,), HID ** -0.5, 0.09375),
        "prior": draw_prior(jax.random.fold_in(key_of[14], 71), 0),
    }


def rows_of(first_core, middle_core, last_core, first_ids, middle_ids, last_ids):
    item_count = first_ids.shape[0]
    first_rows = first_core[first_ids].reshape(item_count, D1, RANK).astype(jnp.float32)
    middle_rows = middle_core[middle_ids].astype(jnp.float32)
    left_part = jnp.einsum("kdr,krm->kdm", first_rows, middle_rows)
    left_part = lax.optimization_barrier(left_part.astype(jnp.bfloat16)).astype(jnp.float32)
    left_part = left_part.reshape(item_count, D1 * D2, RANK)
    last_rows = last_core[last_ids].reshape(item_count, RANK, D3).astype(jnp.float32)
    return jnp.einsum("kar,krd->kad", left_part, last_rows).reshape(item_count, D1 * D2 * D3)


def pooled_table(operands):
    first_core, middle_core, last_core, first_ids, middle_ids, last_ids, lengths = operands

    def pooled_block(block_ids):
        first_block, middle_block, last_block, length_block = block_ids
        row_vecs = rows_of(first_core, middle_core, last_core, first_block.reshape(-1), middle_block.reshape(-1), last_block.reshape(-1))
        row_vecs = row_vecs.reshape(Q_DEV, BAG, D1 * D2 * D3)
        in_bag = (jnp.arange(BAG, dtype=jnp.int32)[None, :] < length_block[:, None]).astype(jnp.float32)
        return jnp.sum(row_vecs * in_bag[:, :, None], axis=1)

    blocks = (first_ids.reshape(-1, Q_DEV, BAG), middle_ids.reshape(-1, Q_DEV, BAG), last_ids.reshape(-1, Q_DEV, BAG), lengths.reshape(-1, Q_DEV))
    return lax.map(pooled_block, blocks).reshape(-1, D1 * D2 * D3)


def reference(core_first, core_middle, core_last, idx_first, idx_middle, idx_last, bag_lengths, cross_down, cross_up, cross_bias, top_weight, top_bias, out_weight, prior):
    batch_rows = REPS * SHARDS * Q_DEV

    def by_table(values):
        return jnp.moveaxis(values.reshape((batch_rows, TABLES) + values.shape[4:]), 1, 0)

    pooled = lax.map(pooled_table, (core_first, core_middle, core_last, by_table(idx_first), by_table(idx_middle), by_table(idx_last), by_table(bag_lengths)))
    x_first = jnp.moveaxis(pooled, 0, 1).reshape(batch_rows, TABLES * D1 * D2 * D3)
    crossed = x_first
    for layer_pos in range(LAYERS):
        low_rank = jnp.dot(crossed.astype(jnp.bfloat16), cross_down[layer_pos], preferred_element_type=jnp.float32).astype(jnp.bfloat16)
        lifted = jnp.dot(low_rank, cross_up[layer_pos], preferred_element_type=jnp.float32)
        crossed = x_first * (lifted + cross_bias[layer_pos].astype(jnp.float32)) + crossed
    hidden = jax.nn.relu(jnp.dot(crossed.astype(jnp.bfloat16), top_weight, preferred_element_type=jnp.float32) + top_bias.astype(jnp.float32)).astype(jnp.bfloat16)
    logits = jnp.dot(hidden, out_weight, preferred_element_type=jnp.float32).reshape(REPS, SHARDS, Q_DEV) + prior
    clicks = jax.nn.sigmoid(logits)
    request_sum = jnp.sum(clicks, axis=(0, 2))
    click_share = (REPS * Q_DEV) * clicks / request_sum[None, :, None]
    return logits, click_share
```

```python
import functools

import jax
import jax.numpy as jnp
from jax import lax
from jax.experimental import pallas as pl
from jax.experimental.pallas import tpu as pltpu
from jax.sharding import PartitionSpec as P

D1 = 8
D2 = 2
D3 = 8
BAG = 2
TILE = 32
LANES = 128

BF16 = jnp.bfloat16
F32 = jnp.float32
I32 = jnp.int32


def iota(shape, dim):
    return lax.broadcasted_iota(I32, shape, dim)


def dot(a, b):
    return jnp.dot(a, b, preferred_element_type=F32)


def dot_nt(a, b):
    return lax.dot_general(a, b, (((1,), (1,)), ((), ())), preferred_element_type=F32)


def order_kernel(groups, first_ref, middle_ref, dest_ref, owner_ref, slot_ref, rank_ref, sums_ref):
    blocks, width = first_ref.shape
    group_row = iota((groups, width), 0)
    before = (iota((width, width), 0) < iota((width, width), 1)).astype(BF16)

    def count(b, seen):
        hot = group_row == middle_ref[pl.ds(b, 1), :]
        ranks = dot(hot.astype(F32).astype(BF16), before)
        rank_ref[pl.ds(b, 1), :] = jnp.sum(jnp.where(hot, ranks + seen, 0.0), axis=0, keepdims=True)
        return seen + jnp.sum(hot.astype(F32), axis=1, keepdims=True)

    counts = lax.fori_loop(0, blocks, count, jnp.zeros((groups, 1), F32))
    tiles = jnp.floor((counts + (TILE - 1)) * (1.0 / TILE))
    tiles = jnp.broadcast_to(tiles, (groups, LANES))
    high = jnp.floor(tiles * (1.0 / 16))
    low = tiles - 16.0 * high
    above = (iota((groups, groups), 0) > iota((groups, groups), 1)).astype(BF16)
    offset = 16.0 * dot(above, high.astype(BF16)) + dot(above, low.astype(BF16))
    offset = offset[:, :1]
    tile_lane = iota((groups, owner_ref.shape[1]), 1)
    owner_ref[...] = jnp.sum((offset.astype(I32) <= tile_lane).astype(I32), axis=0, keepdims=True) - 1

    sums_ref[...] = jnp.zeros_like(sums_ref)
    lane_row = iota((LANES, width), 0)

    def place(b, carry):
        hot = group_row == middle_ref[pl.ds(b, 1), :]
        start = jnp.sum(jnp.where(hot, offset, 0.0), axis=0, keepdims=True) * TILE
        dest = (rank_ref[pl.ds(b, 1), :] + start).astype(I32)
        dest_ref[pl.ds(b, 1), :] = dest
        ids = first_ref[pl.ds(b, 1), :]
        at_lane = lane_row == (dest & (LANES - 1))
        high_id = jnp.where(at_lane, (ids >> 4).astype(F32), 0.0)
        low_id = jnp.where(at_lane, (ids & 15).astype(F32), 0.0)
        at_block = (lane_row == (dest >> 7)).astype(F32).astype(BF16)
        sums_ref[...] += dot_nt(jnp.concatenate([high_id, low_id], axis=0).astype(BF16), at_block)
        return carry

    lax.fori_loop(0, blocks, place, 0)
    slot_ref[...] = (16.0 * sums_ref[:LANES, :] + sums_ref[LANES:, :]).astype(I32)


def order(first_ids, middle_ids, groups):
    items = first_ids.size
    width = 256
    most_tiles = items // TILE + groups
    owners = -(-most_tiles // LANES) * LANES
    return pl.pallas_call(
        functools.partial(order_kernel, groups),
        out_shape=(
            jax.ShapeDtypeStruct((items // width, width), I32),
            jax.ShapeDtypeStruct((1, owners), I32),
            jax.ShapeDtypeStruct((LANES, LANES), I32),
        ),
        scratch_shapes=[
            pltpu.VMEM((items // width, width), F32),
            pltpu.VMEM((2 * LANES, LANES), F32),
        ],
        cost_estimate=pl.CostEstimate(flops=int(2e9), bytes_accessed=200000, transcendentals=0),
        name="order",
    )(first_ids.reshape(-1, width), middle_ids.reshape(-1, width))


def lookup_kernel(
    items,
    dest_ref,
    owner_ref,
    slot_ref,
    last_ids_ref,
    first_ref,
    middle_ref,
    last_ref,
    out_ref,
    pair_ref,
    last_by_d3_ref,
    left_ref,
    spread_ref,
    last_rows_ref,
    staged_ref,
    diag_ref,
):
    queries = items // BAG
    groups, rank, wide = middle_ref.shape
    rows, first_width = first_ref.shape

    def make_pair(g, carry):
        core = middle_ref[pl.ds(g, 1)].reshape(rank, wide)
        zero = jnp.zeros_like(core)
        pair_ref[pl.ds(g, 1), :rank, :wide] = core.reshape(1, rank, wide)
        pair_ref[pl.ds(g, 1), :rank, wide:] = zero.reshape(1, rank, wide)
        pair_ref[pl.ds(g, 1), rank:, :wide] = zero.reshape(1, rank, wide)
        pair_ref[pl.ds(g, 1), rank:, wide:] = core.reshape(1, rank, wide)
        return carry

    lax.fori_loop(0, groups, make_pair, 0)
    width = last_ref.shape[1]
    from_row, to_lane = iota((width, width), 0), iota((width, width), 1)
    swap = (to_lane == (from_row & (D3 - 1)) * rank + (from_row >> 3)).astype(F32).astype(BF16)
    last_by_d3_ref[...] = dot(last_ref[...], swap).astype(BF16)

    per_step = LANES // TILE
    steps = -(-(items // TILE + groups) // per_step)
    slot_lane = iota((LANES, LANES), 1)
    row_lane = iota((LANES, rows), 1)

    def make_left(step, carry):
        ids = jnp.sum(jnp.where(slot_lane == step, slot_ref[...], 0), axis=1, keepdims=True)
        hot = (row_lane == ids).astype(F32).astype(BF16)
        cores = dot(hot, first_ref[...]).astype(BF16)
        for t in range(per_step):
            owner = owner_ref[0, step * per_step + t]
            rows_t = cores[t * TILE : (t + 1) * TILE]
            stacked = jnp.concatenate(
                [rows_t[:, p * LANES : (p + 1) * LANES] for p in range(D1 // 2)], axis=0
            )
            pair = pair_ref[pl.ds(owner, 1)].reshape(2 * rank, 2 * wide)
            product = dot(stacked, pair)
            for p in range(D1 // 2):
                for half in range(2):
                    for s in range(TILE // 8):
                        spread_ref[t, pl.ds(s * 64 + 2 * p + half, 8, stride=D1), :] = product[
                            p * TILE + s * 8 : p * TILE + s * 8 + 8, half * wide : (half + 1) * wide
                        ]
            left_ref[pl.ds((step * per_step + t) * TILE, TILE)] = (
                spread_ref[t].reshape(TILE, D1, wide).astype(BF16)
            )
        return carry

    lax.fori_loop(0, steps, make_left, 0)

    group = TILE
    per_block = LANES // group
    blocks = queries // LANES
    id_lane = iota(last_ids_ref.shape, 1)
    low_half = iota((group, LANES), 1) < rank
    own = (iota((group, LANES), 1) >> 3) == (iota((group, LANES), 0) & 15)
    taps = D2 * D3 * LANES
    tap, spot = iota((taps, LANES), 0), iota((taps, LANES), 1)
    gather_own = (spot == (tap & (D1 - 1)) * (D2 * D3) + (tap >> 7)).astype(F32).astype(BF16)

    def make_block(block, carry):
        for k in range(BAG):
            ids = jnp.sum(
                jnp.where(id_lane == k * blocks + block, last_ids_ref[...], 0), axis=1, keepdims=True
            )
            hot = (row_lane == ids).astype(F32).astype(BF16)
            last_rows_ref[k] = dot(hot, last_by_d3_ref[...])

        def make_group(part, inner):
            base = block * LANES + part * group
            for k in range(BAG):
                for q in range(group):
                    at = dest_ref[k * queries + base + q]
                    staged_ref[k, pl.ds(q, 1)] = left_ref[pl.ds(at, 1)]
            right = jnp.concatenate(
                [staged_ref[k].reshape(group * D1, wide) for k in range(BAG)], axis=1
            )
            pieces = [[None] * BAG for _ in range(D2 * D3)]
            for k in range(BAG):
                for tile in range(D3 // 2):
                    both = last_rows_ref[k, pl.ds(part * group, group), tile * LANES : (tile + 1) * LANES]
                    low = jnp.where(low_half, both, 0.0)
                    high = jnp.where(low_half, 0.0, both)
                    pieces[2 * tile][k] = low
                    pieces[D3 + 2 * tile][k] = pltpu.roll(low, rank, 1)
                    pieces[2 * tile + 1][k] = pltpu.roll(high, rank, 1)
                    pieces[D3 + 2 * tile + 1][k] = high
            lasts = jnp.concatenate(
                [jnp.concatenate(p, axis=1) for p in pieces], axis=0
            ).astype(BF16)
            product = dot_nt(lasts, right)
            for e in range(D2 * D3):
                at = e * group
                mine = jnp.concatenate(
                    [product[at : at + 16, :LANES], product[at + 16 : at + 32, LANES:]], axis=0
                )
                diag_ref[pl.ds(part * group, group), e * LANES : (e + 1) * LANES] = jnp.where(
                    own, mine, 0.0
                ).astype(BF16)
            return inner

        lax.fori_loop(0, per_block, make_group, 0)
        out_ref[pl.ds(block * LANES, LANES), :] = dot(diag_ref[...], gather_own).astype(BF16)
        return carry

    lax.fori_loop(0, blocks, make_block, 0)


def lookup(dest, owner, slot, last_ids, core_first, core_middle, core_last):
    items = dest.size
    groups, rank, wide = core_middle.shape
    slots = -(-(items // TILE + groups) // (LANES // TILE)) * LANES
    smem = pl.BlockSpec(memory_space=pltpu.SMEM)
    vmem = pl.BlockSpec(memory_space=pltpu.VMEM)
    return pl.pallas_call(
        functools.partial(lookup_kernel, items),
        out_shape=jax.ShapeDtypeStruct((items // BAG, LANES), BF16),
        in_specs=[smem, smem, vmem, vmem, vmem, vmem, vmem],
        out_specs=vmem,
        scratch_shapes=[
            pltpu.VMEM((groups, 2 * rank, 2 * wide), BF16),
            pltpu.VMEM(core_last.shape, BF16),
            pltpu.VMEM((slots, D1, wide), BF16),
            pltpu.VMEM((LANES // TILE, TILE * D1, wide), F32),
            pltpu.VMEM((BAG, LANES, core_last.shape[1]), F32),
            pltpu.VMEM((BAG, TILE, D1, wide), BF16),
            pltpu.VMEM((LANES, D2 * D3 * LANES), BF16),
        ],
        compiler_params=pltpu.CompilerParams(vmem_limit_bytes=56 * 2**20),
        cost_estimate=pl.CostEstimate(flops=int(60e9), bytes_accessed=5000000, transcendentals=0),
        name="lookup",
    )(dest.reshape(-1), owner, slot, last_ids, core_first, core_middle, core_last)


def top_kernel(
    core_ref, recv_ref, own_ref, other_ref, down_ref, up_ref, bias_ref, top_bias_ref, out_weight_ref,
    logit_ref, first_half_ref, second_half_ref, sum_ref,
):
    step = pl.program_id(0)
    depth = own_ref.shape[1]

    @pl.when(step == 0)
    def _():
        first = jnp.concatenate(
            [recv_ref[t] for t in range(recv_ref.shape[0])], axis=1
        ).astype(F32)
        crossed = first
        for layer in range(down_ref.shape[0]):
            low = dot(crossed.astype(BF16), down_ref[layer]).astype(BF16)
            lifted = dot(low, up_ref[layer])
            crossed = first * (lifted + bias_ref[layer : layer + 1, :].astype(F32)) + crossed
        crossed = crossed.astype(BF16)
        swap = core_ref[0] == 1

        @pl.when(swap)
        def _():
            first_half_ref[...] = crossed[:, depth:]
            second_half_ref[...] = crossed[:, :depth]

        @pl.when(jnp.logical_not(swap))
        def _():
            first_half_ref[...] = crossed[:, :depth]
            second_half_ref[...] = crossed[:, depth:]

        sum_ref[...] = jnp.zeros_like(sum_ref)

    hidden = dot(first_half_ref[...], own_ref[0]) + dot(second_half_ref[...], other_ref[0])
    hidden = jnp.maximum(hidden + top_bias_ref[0].astype(F32), 0.0).astype(BF16).astype(F32)
    sum_ref[...] += hidden * out_weight_ref[0].astype(F32)

    @pl.when(step == pl.num_programs(0) - 1)
    def _():
        logit_ref[...] = jnp.sum(sum_ref[...], axis=1, keepdims=True)


def top(core, received, own, other, cross_down, cross_up, cross_bias, top_bias, out_weight):
    shards, depth, hid = own.shape
    queries = received.shape[1]

    def whole(shape):
        return pl.BlockSpec(shape, lambda t: (0,) * len(shape))

    return pl.pallas_call(
        top_kernel,
        grid=(shards,),
        out_shape=jax.ShapeDtypeStruct((queries, 1), F32),
        in_specs=[
            pl.BlockSpec(memory_space=pltpu.SMEM),
            whole(received.shape),
            pl.BlockSpec((1, depth, hid), lambda t: (t, 0, 0)),
            pl.BlockSpec((1, depth, hid), lambda t: (t, 0, 0)),
            whole(cross_down.shape),
            whole(cross_up.shape),
            whole(cross_bias.shape),
            pl.BlockSpec((1, 1, hid), lambda t: (t, 0, 0)),
            pl.BlockSpec((1, 1, hid), lambda t: (t, 0, 0)),
        ],
        out_specs=whole((queries, 1)),
        scratch_shapes=[
            pltpu.VMEM((queries, depth), BF16),
            pltpu.VMEM((queries, depth), BF16),
            pltpu.VMEM((queries, hid), F32),
        ],
        compiler_params=pltpu.CompilerParams(vmem_limit_bytes=56 * 2**20),
        cost_estimate=pl.CostEstimate(flops=int(8e9), bytes_accessed=24000000, transcendentals=0),
        name="top",
    )(
        core, received, own, other, cross_down, cross_up, cross_bias,
        top_bias.reshape(shards, 1, hid), out_weight.reshape(shards, 1, hid),
    )


def body(
    core_first,
    core_middle,
    core_last,
    idx_first,
    idx_middle,
    idx_last,
    bag_lengths,
    cross_down,
    cross_up,
    cross_bias,
    top_weight,
    top_bias,
    out_weight,
    prior,
):
    shards = lax.axis_size("tables")
    replicas = lax.axis_size("replica")
    queries = idx_first.shape[2]

    core = lax.rem(lax.axis_index("replica"), 2)
    depth = top_weight.shape[0] // 2
    part = lax.dynamic_slice_in_dim(top_weight, core * depth, depth, axis=0)
    own = lax.all_gather(part, "tables", axis=0)
    other = lax.ppermute(own, "replica", [(i, i ^ 1) for i in range(replicas)])

    in_bag = jnp.arange(BAG, dtype=I32)[None, :, None] < bag_lengths[0, 0].T[:, None, :]

    def by_table(values):
        return jnp.transpose(values[0, 0], (1, 2, 0))

    sent = jnp.concatenate(
        [
            by_table(idx_first),
            by_table(idx_middle),
            jnp.where(in_bag, by_table(idx_last), -1),
        ],
        axis=1,
    )
    at_owner = lax.all_to_all(sent, "tables", split_axis=0, concat_axis=0, tiled=True)
    at_owner = jnp.transpose(at_owner, (1, 0, 2))
    first_ids, middle_ids, last_ids = (
        at_owner[BAG * i : BAG * (i + 1)].reshape(-1, LANES) for i in range(3)
    )
    dest, owner, slot = order(first_ids, middle_ids, core_middle.shape[1])
    pooled = lookup(
        dest, owner, slot, last_ids.T, core_first[0], core_middle[0], core_last[0]
    )
    received = lax.all_to_all(
        pooled.reshape(shards, queries, LANES), "tables", split_axis=0, concat_axis=0, tiled=True
    )
    summed = top(
        core.reshape(1), received, own, other, cross_down, cross_up, cross_bias, top_bias, out_weight
    )
    logits = summed[:, 0] + prior[0, 0]
    clicks = jax.nn.sigmoid(logits)
    request_sum = lax.psum(jnp.sum(clicks), "replica")
    click_share = replicas * queries * clicks / request_sum
    return (logits[None, None], click_share[None, None])


def solution(mesh):
    in_specs = (
        P("tables", None, None),
        P("tables", None, None, None),
        P("tables", None, None),
        P("replica", "tables", None, None, None),
        P("replica", "tables", None, None, None),
        P("replica", "tables", None, None, None),
        P("replica", "tables", None, None),
        P(),
        P(),
        P(),
        P(None, "tables"),
        P(),
        P(),
        P("replica", "tables", None),
    )
    out_specs = (P("replica", "tables", None), P("replica", "tables", None))
    return jax.shard_map(body, mesh=mesh, in_specs=in_specs, out_specs=out_specs, check_vma=False)
```

```python
import functools

import jax
import jax.numpy as jnp
from jax import lax
from jax.experimental import pallas as pl
from jax.experimental.pallas import tpu as pltpu
from jax.sharding import PartitionSpec as P

D1 = 8
D2 = 2
D3 = 8
BAG = 2
TILE = 32
LANES = 128
STEP = 512

BF16 = jnp.bfloat16
F32 = jnp.float32
I32 = jnp.int32
MESH = pl.DeviceIdType.MESH


def iota(shape, dim):
    return lax.broadcasted_iota(I32, shape, dim)


def dot(a, b):
    return jnp.dot(a, b, preferred_element_type=F32)


def dot_nt(a, b):
    return lax.dot_general(a, b, (((1,), (1,)), ((), ())), preferred_element_type=F32)


def order_kernel(groups, first_ref, middle_ref, dest_ref, owner_ref, slot_ref, rank_ref, sums_ref):
    blocks, width = first_ref.shape
    group_row = iota((groups, width), 0)
    before = (iota((width, width), 0) < iota((width, width), 1)).astype(BF16)
    together = 8

    def hot_rows(first):
        ids = middle_ref[pl.ds(first, together), :]
        return [group_row == ids[u : u + 1, :] for u in range(together)]

    def count(step, seen):
        hots = hot_rows(step * together)
        ones = jnp.concatenate([h.astype(F32) for h in hots], axis=0)
        ranks = dot(ones.astype(BF16), before)
        sizes = jnp.sum(ones, axis=1, keepdims=True)
        rows = []
        for u in range(together):
            at = slice(u * groups, (u + 1) * groups)
            rows.append(jnp.sum(jnp.where(hots[u], ranks[at] + seen, 0.0), axis=0, keepdims=True))
            seen = seen + sizes[at]
        rank_ref[pl.ds(step * together, together), :] = jnp.concatenate(rows, axis=0)
        return seen

    counts = lax.fori_loop(0, blocks // together, count, jnp.zeros((groups, 1), F32))
    tiles = jnp.floor((counts + (TILE - 1)) * (1.0 / TILE))
    tiles = jnp.broadcast_to(tiles, (groups, LANES))
    high = jnp.floor(tiles * (1.0 / 16))
    low = tiles - 16.0 * high
    above = (iota((groups, groups), 0) > iota((groups, groups), 1)).astype(BF16)
    offset = 16.0 * dot(above, high.astype(BF16)) + dot(above, low.astype(BF16))
    offset = offset[:, :1]
    tile_lane = iota((groups, owner_ref.shape[1]), 1)
    owner_ref[...] = jnp.sum((offset.astype(I32) <= tile_lane).astype(I32), axis=0, keepdims=True) - 1

    sums_ref[...] = jnp.zeros_like(sums_ref)
    lane_row = iota((LANES, width), 0)

    def place(step, carry):
        first = step * together
        hots = hot_rows(first)
        starts = [jnp.sum(jnp.where(h, offset, 0.0), axis=0, keepdims=True) for h in hots]
        dests = (rank_ref[pl.ds(first, together), :] + TILE * jnp.concatenate(starts, axis=0)).astype(I32)
        dest_ref[pl.ds(first, together), :] = dests
        ids = first_ref[pl.ds(first, together), :]
        lanes, highs, lows, rows = dests & (LANES - 1), (ids >> 4).astype(F32), (ids & 15).astype(F32), dests >> 7
        values, spots = [], []
        for u in range(together):
            at = slice(u, u + 1)
            at_lane = lane_row == lanes[at]
            values.append(
                jnp.concatenate(
                    [jnp.where(at_lane, highs[at], 0.0), jnp.where(at_lane, lows[at], 0.0)], axis=0
                ).astype(BF16)
            )
            spots.append((lane_row == rows[at]).astype(F32).astype(BF16))
        sums_ref[...] += dot_nt(jnp.concatenate(values, axis=1), jnp.concatenate(spots, axis=1))
        return carry

    lax.fori_loop(0, blocks // together, place, 0)
    slot_ref[...] = (16.0 * sums_ref[:LANES, :] + sums_ref[LANES:, :]).astype(I32)


def order(first_ids, middle_ids, groups):
    items = first_ids.size
    width = 256
    most_tiles = items // TILE + groups
    owners = -(-most_tiles // LANES) * LANES
    return pl.pallas_call(
        functools.partial(order_kernel, groups),
        out_shape=(
            jax.ShapeDtypeStruct((items // width, width), I32),
            jax.ShapeDtypeStruct((1, owners), I32),
            jax.ShapeDtypeStruct((LANES, LANES), I32),
        ),
        scratch_shapes=[
            pltpu.VMEM((items // width, width), F32),
            pltpu.VMEM((2 * LANES, LANES), F32),
        ],
        cost_estimate=pl.CostEstimate(flops=int(2e9), bytes_accessed=200000, transcendentals=0),
        name="order",
    )(first_ids.reshape(-1, width), middle_ids.reshape(-1, width))


def lookup_kernel(
    items,
    dest_ref,
    owner_ref,
    slot_ref,
    last_ids_ref,
    first_ref,
    middle_ref,
    last_ref,
    out_ref,
    pair_ref,
    last_by_d3_ref,
    left_ref,
    spread_ref,
    cores_a_ref,
    cores_b_ref,
    last_a_ref,
    last_b_ref,
    staged_ref,
    diag_a_ref,
    diag_b_ref,
    gather_own_ref,
):
    queries = items // BAG
    groups, rank, wide = middle_ref.shape
    rows, first_width = first_ref.shape

    def make_pair(g, carry):
        core = middle_ref[pl.ds(g, 1)].reshape(rank, wide)
        zero = jnp.zeros_like(core)
        pair_ref[pl.ds(g, 1), :rank, :wide] = core.reshape(1, rank, wide)
        pair_ref[pl.ds(g, 1), :rank, wide:] = zero.reshape(1, rank, wide)
        pair_ref[pl.ds(g, 1), rank:, :wide] = zero.reshape(1, rank, wide)
        pair_ref[pl.ds(g, 1), rank:, wide:] = core.reshape(1, rank, wide)
        return carry

    lax.fori_loop(0, groups, make_pair, 0)
    width = last_ref.shape[1]
    from_row, to_lane = iota((width, width), 0), iota((width, width), 1)
    swap = (to_lane == (from_row & (D3 - 1)) * rank + (from_row >> 3)).astype(F32).astype(BF16)
    last_by_d3_ref[...] = dot(last_ref[...], swap).astype(BF16)

    per_step = STEP // TILE
    pairs = left_ref.shape[0] // (2 * STEP)
    slot_lane = iota((LANES, LANES), 1)
    row_lane = iota((LANES, rows), 1)

    def hot_of(ids):
        return (row_lane == ids).astype(F32).astype(BF16)

    def gather_first(step, to_ref):
        hots = []
        for c in range(STEP // LANES):
            column = step * (STEP // LANES) + c
            hots.append(
                hot_of(jnp.sum(jnp.where(slot_lane == column, slot_ref[...], 0), axis=1, keepdims=True))
            )
        to_ref[...] = dot(jnp.concatenate(hots, axis=0), first_ref[...]).astype(BF16)

    def make_left(step, from_ref):
        for t in range(per_step):
            owner = owner_ref[0, step * per_step + t]
            stacked = jnp.concatenate(
                [
                    from_ref[t * TILE : (t + 1) * TILE, p * LANES : (p + 1) * LANES]
                    for p in range(D1 // 2)
                ],
                axis=0,
            )
            pair = pair_ref[pl.ds(owner, 1)].reshape(2 * rank, 2 * wide)
            product = dot(stacked, pair)
            for p in range(D1 // 2):
                for half in range(2):
                    for s in range(TILE // 8):
                        spread_ref[t, pl.ds(s * 64 + 2 * p + half, 8, stride=D1), :] = product[
                            p * TILE + s * 8 : p * TILE + s * 8 + 8, half * wide : (half + 1) * wide
                        ]
            left_ref[pl.ds((step * per_step + t) * TILE, TILE)] = (
                spread_ref[t].reshape(TILE, D1, wide).astype(BF16)
            )

    gather_first(0, cores_a_ref)

    def left_pair(pair, carry):
        gather_first(2 * pair + 1, cores_b_ref)
        make_left(2 * pair, cores_a_ref)
        gather_first(2 * pair + 2, cores_a_ref)
        make_left(2 * pair + 1, cores_b_ref)
        return carry

    lax.fori_loop(0, pairs, left_pair, 0)

    group = TILE
    per_block = LANES // group
    blocks = queries // LANES
    id_lane = iota(last_ids_ref.shape, 1)
    low_half = iota((group, LANES), 1) < rank
    own = (iota((group, LANES), 1) >> 3) == (iota((group, LANES), 0) & 15)
    taps = D2 * D3 * LANES
    tap, spot = iota((taps, LANES), 0), iota((taps, LANES), 1)
    gather_own_ref[...] = (spot == (tap & (D1 - 1)) * (D2 * D3) + (tap >> 7)).astype(F32).astype(BF16)

    def gather_last(block, to_ref):
        hots = [
            hot_of(
                jnp.sum(
                    jnp.where(id_lane == k * blocks + block, last_ids_ref[...], 0), axis=1, keepdims=True
                )
            )
            for k in range(BAG)
        ]
        to_ref[...] = dot(jnp.concatenate(hots, axis=0), last_by_d3_ref[...])

    def make_group(block, part, which, from_ref, diag_ref):
        base = block * LANES + part * group
        for k in range(BAG):
            for q in range(group):
                at = dest_ref[k * queries + base + q]
                staged_ref[which, k, q] = left_ref[at]
        right = jnp.concatenate(
            [staged_ref[which, k].reshape(group * D1, wide) for k in range(BAG)], axis=1
        )
        pieces = [[None] * BAG for _ in range(D2 * D3)]
        for k in range(BAG):
            start = k * LANES + part * group
            for tile in range(D3 // 2):
                both = from_ref[start : start + group, tile * LANES : (tile + 1) * LANES]
                low = jnp.where(low_half, both, 0.0)
                high = jnp.where(low_half, 0.0, both)
                pieces[2 * tile][k] = low
                pieces[D3 + 2 * tile][k] = pltpu.roll(low, rank, 1)
                pieces[2 * tile + 1][k] = pltpu.roll(high, rank, 1)
                pieces[D3 + 2 * tile + 1][k] = high
        lasts = jnp.concatenate([jnp.concatenate(p, axis=1) for p in pieces], axis=0).astype(BF16)
        product = dot_nt(lasts, right)
        for e in range(D2 * D3):
            at = e * group
            mine = jnp.concatenate(
                [product[at : at + 16, :LANES], product[at + 16 : at + 32, LANES:]], axis=0
            )
            diag_ref[part * group : (part + 1) * group, e * LANES : (e + 1) * LANES] = jnp.where(
                own, mine, 0.0
            ).astype(BF16)

    def make_block(block, which, from_ref, diag_ref):
        for part in range(per_block):
            make_group(block, part, which + part, from_ref, diag_ref)
        out_ref[pl.ds(block * LANES, LANES), :] = dot(diag_ref[...], gather_own_ref[...]).astype(BF16)

    gather_last(0, last_a_ref)

    def block_pair(pair, carry):
        gather_last(2 * pair + 1, last_b_ref)
        make_block(2 * pair, 0, last_a_ref, diag_a_ref)
        gather_last(jnp.minimum(2 * pair + 2, blocks - 1), last_a_ref)
        make_block(2 * pair + 1, per_block, last_b_ref, diag_b_ref)
        return carry

    lax.fori_loop(0, blocks // 2, block_pair, 0)


def lookup(dest, owner, slot, last_ids, core_first, core_middle, core_last):
    items = dest.size
    groups, rank, wide = core_middle.shape
    slots = -(-(items + groups * TILE) // (2 * STEP)) * 2 * STEP
    smem = pl.BlockSpec(memory_space=pltpu.SMEM)
    vmem = pl.BlockSpec(memory_space=pltpu.VMEM)
    return pl.pallas_call(
        functools.partial(lookup_kernel, items),
        out_shape=jax.ShapeDtypeStruct((items // BAG, LANES), BF16),
        in_specs=[smem, smem, vmem, vmem, vmem, vmem, vmem],
        out_specs=vmem,
        scratch_shapes=[
            pltpu.VMEM((groups, 2 * rank, 2 * wide), BF16),
            pltpu.VMEM(core_last.shape, BF16),
            pltpu.VMEM((slots, D1, wide), BF16),
            pltpu.VMEM((STEP // TILE, TILE * D1, wide), F32),
            pltpu.VMEM((STEP, core_first.shape[1]), BF16),
            pltpu.VMEM((STEP, core_first.shape[1]), BF16),
            pltpu.VMEM((BAG * LANES, core_last.shape[1]), F32),
            pltpu.VMEM((BAG * LANES, core_last.shape[1]), F32),
            pltpu.VMEM((2 * LANES // TILE, BAG, TILE, D1, wide), BF16),
            pltpu.VMEM((LANES, D2 * D3 * LANES), BF16),
            pltpu.VMEM((LANES, D2 * D3 * LANES), BF16),
            pltpu.VMEM((D2 * D3 * LANES, LANES), BF16),
        ],
        compiler_params=pltpu.CompilerParams(vmem_limit_bytes=56 * 2**20),
        cost_estimate=pl.CostEstimate(flops=int(60e9), bytes_accessed=5000000, transcendentals=0),
        name="lookup",
    )(dest.reshape(-1), owner, slot, last_ids, core_first, core_middle, core_last)


def tail_kernel(
    pooled_ref, weight_ref, down_ref, up_ref, bias_ref, top_bias_ref, out_weight_ref, prior_ref,
    logit_ref, share_ref,
    recv_ref, mine_ref, theirs_ref, wide_ref, down_v, up_v, part_ref, part_in_ref, click_ref, sum_ref,
    pooled_send, pooled_recv, local_sem, weight_sem, pair_send, pair_recv, part_send, part_recv,
    click_send, click_recv,
):
    shards, queries, lanes = pooled_ref.shape
    replicas = lax.axis_size("replica")
    me, rep = lax.axis_index("tables"), lax.axis_index("replica")
    sibling = rep + 1 - 2 * lax.rem(rep, 2)

    fetches = [
        pltpu.make_async_copy(down_ref, down_v, weight_sem.at[0]),
        pltpu.make_async_copy(up_ref, up_v, weight_sem.at[1]),
        pltpu.make_async_copy(weight_ref, wide_ref, weight_sem.at[2]),
    ]
    for fetch in fetches:
        fetch.start()
    keep = pltpu.make_async_copy(pooled_ref.at[me], recv_ref.at[me], local_sem)
    keep.start()

    barrier = pltpu.get_barrier_semaphore()
    for i in range(1, shards):
        pl.semaphore_signal(
            barrier, inc=1, device_id={"tables": lax.rem(me + i, shards)}, device_id_type=MESH
        )
    for i in range(1, replicas):
        pl.semaphore_signal(
            barrier, inc=1, device_id={"replica": lax.rem(rep + i, replicas)}, device_id_type=MESH
        )
    pl.semaphore_wait(barrier, shards + replicas - 2)

    sends = []
    for i in range(1, shards):
        to = lax.rem(me + i, shards)
        sends.append(
            pltpu.make_async_remote_copy(
                src_ref=pooled_ref.at[to],
                dst_ref=recv_ref.at[me],
                send_sem=pooled_send.at[i],
                recv_sem=pooled_recv.at[i],
                device_id={"tables": to},
                device_id_type=MESH,
            )
        )
    for send in sends:
        send.start()
    keep.wait()
    for send in sends:
        send.wait()
    fetches[0].wait()
    fetches[1].wait()

    first = jnp.concatenate([recv_ref[t] for t in range(shards)], axis=1).astype(F32)
    crossed = first
    for layer in range(down_v.shape[0]):
        low = dot(crossed.astype(BF16), down_v[layer]).astype(BF16)
        lifted = dot(low, up_v[layer])
        crossed = first * (lifted + bias_ref[layer : layer + 1, :].astype(F32)) + crossed
    mine_ref[...] = crossed.astype(BF16)
    pair = pltpu.make_async_remote_copy(
        src_ref=mine_ref, dst_ref=theirs_ref, send_sem=pair_send, recv_sem=pair_recv,
        device_id={"replica": sibling}, device_id_type=MESH,
    )
    pair.start()
    fetches[2].wait()

    def summed(rows_ref):
        sum_ref[...] = jnp.zeros_like(sum_ref)

        def step(t, carry):
            weight = jnp.concatenate([wide_ref[2 * t], wide_ref[2 * t + 1]], axis=1)
            hidden = dot(rows_ref[...], weight)
            for half in range(2):
                at = 2 * t + half
                unit = hidden[:, half * lanes : (half + 1) * lanes] + top_bias_ref[pl.ds(at, 1), :]
                unit = jnp.maximum(unit, 0.0).astype(BF16).astype(F32)
                sum_ref[:queries] += unit * out_weight_ref[pl.ds(at, 1), :]
            return carry

        lax.fori_loop(0, shards // 2, step, 0)
        return jnp.sum(jnp.transpose(sum_ref[...]), axis=0, keepdims=True)

    ours = summed(mine_ref)
    pair.wait()
    part_ref[...] = jnp.broadcast_to(summed(theirs_ref), part_ref.shape)
    back = pltpu.make_async_remote_copy(
        src_ref=part_ref, dst_ref=part_in_ref, send_sem=part_send, recv_sem=part_recv,
        device_id={"replica": sibling}, device_id_type=MESH,
    )
    back.start()
    back.wait()
    logits = (ours + part_in_ref[:1])[:, :queries] + prior_ref[...]
    logit_ref[...] = logits
    clicks = 1.0 / (1.0 + jnp.exp(-logits))
    click_ref[0] = jnp.broadcast_to(jnp.sum(clicks, axis=1, keepdims=True), click_ref.shape[1:])
    tells = []
    for i in range(1, replicas):
        tells.append(
            pltpu.make_async_remote_copy(
                src_ref=click_ref.at[0],
                dst_ref=click_ref.at[i],
                send_sem=click_send.at[i],
                recv_sem=click_recv.at[i],
                device_id={"replica": lax.rem(rep + i, replicas)},
                device_id_type=MESH,
            )
        )
    for tell in tells:
        tell.start()
    for tell in tells:
        tell.wait()
    total = click_ref[0]
    for i in range(1, replicas):
        total = total + click_ref[i]
    share_ref[...] = (replicas * queries) * clicks / total[:1, :1]


def tail(pooled, weight, cross_down, cross_up, cross_bias, top_bias, out_weight, prior):
    shards, queries, lanes = pooled.shape
    replicas = lax.axis_size("replica")
    feat = cross_down.shape[1]
    padded = -(-queries // LANES) * LANES
    vmem = pl.BlockSpec(memory_space=pltpu.VMEM)
    anywhere = pl.BlockSpec(memory_space=pl.ANY)
    dma = pltpu.SemaphoreType.DMA
    return pl.pallas_call(
        tail_kernel,
        out_shape=(jax.ShapeDtypeStruct((1, queries), F32),) * 2,
        in_specs=[anywhere, anywhere, anywhere, anywhere, vmem, vmem, vmem, vmem],
        out_specs=(vmem, vmem),
        scratch_shapes=[
            pltpu.VMEM((shards, queries, lanes), BF16),
            pltpu.VMEM((queries, feat), BF16),
            pltpu.VMEM((queries, feat), BF16),
            pltpu.VMEM(weight.shape, BF16),
            pltpu.VMEM(cross_down.shape, BF16),
            pltpu.VMEM(cross_up.shape, BF16),
            pltpu.VMEM((8, padded), F32),
            pltpu.VMEM((8, padded), F32),
            pltpu.VMEM((replicas, 8, LANES), F32),
            pltpu.VMEM((padded, LANES), F32),
            dma((shards,)),
            dma((shards,)),
            dma,
            dma((3,)),
            dma,
            dma,
            dma,
            dma,
            dma((replicas,)),
            dma((replicas,)),
        ],
        compiler_params=pltpu.CompilerParams(
            collective_id=1, has_side_effects=True, vmem_limit_bytes=56 * 2**20
        ),
        cost_estimate=pl.CostEstimate(flops=int(20e9), bytes_accessed=24000000, transcendentals=0),
        name="tail",
    )(pooled, weight, cross_down, cross_up, cross_bias, top_bias, out_weight, prior)


def body(
    core_first,
    core_middle,
    core_last,
    idx_first,
    idx_middle,
    idx_last,
    bag_lengths,
    cross_down,
    cross_up,
    cross_bias,
    top_weight,
    top_bias,
    out_weight,
    prior,
):
    shards = lax.axis_size("tables")
    queries = idx_first.shape[2]

    core = lax.rem(lax.axis_index("replica"), 2)
    half = top_weight.shape[1] // 2
    part = lax.dynamic_slice_in_dim(top_weight, core * half, half, axis=1)
    weight = lax.all_gather(part, "tables", axis=0)

    def my_units(values):
        return lax.dynamic_index_in_dim(values.reshape(shards, 2, half), core, 1, keepdims=False)

    in_bag = jnp.arange(BAG, dtype=I32)[None, :, None] < bag_lengths[0, 0].T[:, None, :]

    def by_table(values):
        return jnp.transpose(values[0, 0], (1, 2, 0))

    sent = jnp.concatenate(
        [
            by_table(idx_first),
            by_table(idx_middle),
            jnp.where(in_bag, by_table(idx_last), -1),
        ],
        axis=1,
    )
    at_owner = lax.all_to_all(sent, "tables", split_axis=0, concat_axis=0, tiled=True)
    at_owner = jnp.transpose(at_owner, (1, 0, 2))
    first_ids, middle_ids, last_ids = (
        at_owner[BAG * i : BAG * (i + 1)].reshape(-1, LANES) for i in range(3)
    )
    dest, owner, slot = order(first_ids, middle_ids, core_middle.shape[1])
    pooled = lookup(
        dest, owner, slot, last_ids.T, core_first[0], core_middle[0], core_last[0]
    )
    logits, click_share = tail(
        pooled.reshape(shards, queries, LANES),
        weight,
        cross_down,
        cross_up,
        cross_bias,
        my_units(top_bias).astype(F32),
        my_units(out_weight).astype(F32),
        prior[0],
    )
    return (logits[None], click_share[None])


def solution(mesh):
    in_specs = (
        P("tables", None, None),
        P("tables", None, None, None),
        P("tables", None, None),
        P("replica", "tables", None, None, None),
        P("replica", "tables", None, None, None),
        P("replica", "tables", None, None, None),
        P("replica", "tables", None, None),
        P(),
        P(),
        P(),
        P(None, "tables"),
        P(),
        P(),
        P("replica", "tables", None),
    )
    out_specs = (P("replica", "tables", None), P("replica", "tables", None))
    return jax.shard_map(body, mesh=mesh, in_specs=in_specs, out_specs=out_specs, check_vma=False)
```

```python
import functools

import jax
import jax.numpy as jnp
from jax import lax
from jax.experimental import pallas as pl
from jax.experimental.pallas import tpu as pltpu
from jax.sharding import PartitionSpec as P

D1 = 8
D2 = 2
D3 = 8
BAG = 2
TILE = 32
LANES = 128
STEP = 512

BF16 = jnp.bfloat16
F32 = jnp.float32
I32 = jnp.int32
MESH = pl.DeviceIdType.MESH


def iota(shape, dim):
    return lax.broadcasted_iota(I32, shape, dim)


def dot(a, b):
    return jnp.dot(a, b, preferred_element_type=F32)


def dot_nt(a, b):
    return lax.dot_general(a, b, (((1,), (1,)), ((), ())), preferred_element_type=F32)


def order_kernel(groups, first_ref, middle_ref, dest_ref, owner_ref, slot_ref, rank_ref, sums_ref):
    blocks, width = first_ref.shape
    group_row = iota((groups, width), 0)
    before = (iota((width, width), 0) < iota((width, width), 1)).astype(BF16)
    together = 8

    def hot_rows(first):
        ids = middle_ref[pl.ds(first, together), :]
        return [group_row == ids[u : u + 1, :] for u in range(together)]

    def count(step, seen):
        hots = hot_rows(step * together)
        ones = jnp.concatenate([h.astype(F32) for h in hots], axis=0)
        ranks = dot(ones.astype(BF16), before)
        sizes = jnp.sum(ones, axis=1, keepdims=True)
        rows = []
        for u in range(together):
            at = slice(u * groups, (u + 1) * groups)
            rows.append(jnp.sum(jnp.where(hots[u], ranks[at] + seen, 0.0), axis=0, keepdims=True))
            seen = seen + sizes[at]
        rank_ref[pl.ds(step * together, together), :] = jnp.concatenate(rows, axis=0)
        return seen

    counts = lax.fori_loop(0, blocks // together, count, jnp.zeros((groups, 1), F32))
    tiles = jnp.floor((counts + (TILE - 1)) * (1.0 / TILE))
    tiles = jnp.broadcast_to(tiles, (groups, LANES))
    high = jnp.floor(tiles * (1.0 / 16))
    low = tiles - 16.0 * high
    above = (iota((groups, groups), 0) > iota((groups, groups), 1)).astype(BF16)
    offset = 16.0 * dot(above, high.astype(BF16)) + dot(above, low.astype(BF16))
    offset = offset[:, :1]
    tile_lane = iota((groups, owner_ref.shape[1]), 1)
    owner_ref[...] = jnp.sum((offset.astype(I32) <= tile_lane).astype(I32), axis=0, keepdims=True) - 1

    sums_ref[...] = jnp.zeros_like(sums_ref)
    lane_row = iota((LANES, width), 0)

    def place(step, carry):
        first = step * together
        hots = hot_rows(first)
        starts = [jnp.sum(jnp.where(h, offset, 0.0), axis=0, keepdims=True) for h in hots]
        dests = (rank_ref[pl.ds(first, together), :] + TILE * jnp.concatenate(starts, axis=0)).astype(I32)
        dest_ref[pl.ds(first, together), :] = dests
        ids = first_ref[pl.ds(first, together), :]
        lanes, highs, lows, rows = dests & (LANES - 1), (ids >> 4).astype(F32), (ids & 15).astype(F32), dests >> 7
        values, spots = [], []
        for u in range(together):
            at = slice(u, u + 1)
            at_lane = lane_row == lanes[at]
            values.append(
                jnp.concatenate(
                    [jnp.where(at_lane, highs[at], 0.0), jnp.where(at_lane, lows[at], 0.0)], axis=0
                ).astype(BF16)
            )
            spots.append((lane_row == rows[at]).astype(F32).astype(BF16))
        sums_ref[...] += dot_nt(jnp.concatenate(values, axis=1), jnp.concatenate(spots, axis=1))
        return carry

    lax.fori_loop(0, blocks // together, place, 0)
    slot_ref[...] = (16.0 * sums_ref[:LANES, :] + sums_ref[LANES:, :]).astype(I32)


def order(first_ids, middle_ids, groups):
    items = first_ids.size
    width = 256
    most_tiles = items // TILE + groups
    owners = -(-most_tiles // LANES) * LANES
    return pl.pallas_call(
        functools.partial(order_kernel, groups),
        out_shape=(
            jax.ShapeDtypeStruct((items // width, width), I32),
            jax.ShapeDtypeStruct((1, owners), I32),
            jax.ShapeDtypeStruct((LANES, LANES), I32),
        ),
        scratch_shapes=[
            pltpu.VMEM((items // width, width), F32),
            pltpu.VMEM((2 * LANES, LANES), F32),
        ],
        cost_estimate=pl.CostEstimate(flops=int(2e9), bytes_accessed=200000, transcendentals=0),
        name="order",
    )(first_ids.reshape(-1, width), middle_ids.reshape(-1, width))


def main_kernel(
    items,
    dest_ref, owner_ref, slot_ref, last_ids_ref, first_ref, middle_ref, last_ref,
    weight_ref, down_ref, up_ref, bias_ref, top_bias_ref, out_weight_ref, prior_ref,
    both_ref,
    pair_ref, last_by_d3_ref, left_ref, spread_ref, cores_a_ref, cores_b_ref, last_a_ref, last_b_ref,
    staged_ref, diag_a_ref, diag_b_ref, gather_own_ref,
    out_ref, recv_ref, mine_ref, theirs_ref, down_v, up_v, part_ref, part_in_ref, click_ref, sum_ref,
    pooled_send, pooled_recv, weight_sem, pair_send, pair_recv, part_send, part_recv,
    click_send, click_recv,
):
    shards, mine, lanes = recv_ref.shape
    replicas = lax.axis_size("replica")
    me, rep = lax.axis_index("tables"), lax.axis_index("replica")
    sibling = rep + 1 - 2 * lax.rem(rep, 2)
    barrier = pltpu.get_barrier_semaphore()
    for i in range(1, shards):
        pl.semaphore_signal(
            barrier, inc=1, device_id={"tables": lax.rem(me + i, shards)}, device_id_type=MESH
        )
    for i in range(1, replicas):
        pl.semaphore_signal(
            barrier, inc=1, device_id={"replica": lax.rem(rep + i, replicas)}, device_id_type=MESH
        )
    fetches = [
        pltpu.make_async_copy(down_ref, down_v, weight_sem.at[0]),
        pltpu.make_async_copy(up_ref, up_v, weight_sem.at[1]),
        pltpu.make_async_copy(weight_ref, left_ref.at[pl.ds(0, weight_ref.shape[0])], weight_sem.at[2]),
    ]
    fetches[0].start()
    fetches[1].start()

    queries = items // BAG
    groups, rank, wide = middle_ref.shape
    rows, first_width = first_ref.shape

    def make_pair(g, carry):
        core = middle_ref[pl.ds(g, 1)].reshape(rank, wide)
        zero = jnp.zeros_like(core)
        pair_ref[pl.ds(g, 1), :rank, :wide] = core.reshape(1, rank, wide)
        pair_ref[pl.ds(g, 1), :rank, wide:] = zero.reshape(1, rank, wide)
        pair_ref[pl.ds(g, 1), rank:, :wide] = zero.reshape(1, rank, wide)
        pair_ref[pl.ds(g, 1), rank:, wide:] = core.reshape(1, rank, wide)
        return carry

    lax.fori_loop(0, groups, make_pair, 0)
    width = last_ref.shape[1]
    from_row, to_lane = iota((width, width), 0), iota((width, width), 1)
    swap = (to_lane == (from_row & (D3 - 1)) * rank + (from_row >> 3)).astype(F32).astype(BF16)
    last_by_d3_ref[...] = dot(last_ref[...], swap).astype(BF16)

    per_step = STEP // TILE
    pairs = left_ref.shape[0] // (2 * STEP)
    slot_lane = iota((LANES, LANES), 1)

    def hot_of(ids):
        return (iota((ids.shape[0], rows), 1) == ids).astype(F32).astype(BF16)

    def gather_first(step, to_ref):
        hots = []
        for c in range(STEP // LANES):
            column = step * (STEP // LANES) + c
            hots.append(
                hot_of(jnp.sum(jnp.where(slot_lane == column, slot_ref[...], 0), axis=1, keepdims=True))
            )
        to_ref[...] = dot(jnp.concatenate(hots, axis=0), first_ref[...]).astype(BF16)

    def make_left(step, from_ref):
        for t in range(per_step):
            owner = owner_ref[0, step * per_step + t]
            stacked = jnp.concatenate(
                [
                    from_ref[t * TILE : (t + 1) * TILE, p * LANES : (p + 1) * LANES]
                    for p in range(D1 // 2)
                ],
                axis=0,
            )
            pair = pair_ref[pl.ds(owner, 1)].reshape(2 * rank, 2 * wide)
            product = dot(stacked, pair)
            for p in range(D1 // 2):
                for half in range(2):
                    for s in range(TILE // 8):
                        spread_ref[t, pl.ds(s * 64 + 2 * p + half, 8, stride=D1), :] = product[
                            p * TILE + s * 8 : p * TILE + s * 8 + 8, half * wide : (half + 1) * wide
                        ]
            left_ref[pl.ds((step * per_step + t) * TILE, TILE)] = (
                spread_ref[t].reshape(TILE, D1, wide).astype(BF16)
            )

    gather_first(0, cores_a_ref)

    def left_pair(pair, carry):
        gather_first(2 * pair + 1, cores_b_ref)
        make_left(2 * pair, cores_a_ref)
        gather_first(2 * pair + 2, cores_a_ref)
        make_left(2 * pair + 1, cores_b_ref)
        return carry

    lax.fori_loop(0, pairs, left_pair, 0)

    group = TILE
    unit = last_ids_ref.shape[0]
    units = mine // unit
    per_unit = unit // group
    id_lane = iota(last_ids_ref.shape, 1)
    low_half = iota((group, LANES), 1) < rank
    own = (iota((group, LANES), 1) >> 3) == (iota((group, LANES), 0) & 15)
    taps = D2 * D3 * LANES
    tap, spot = iota((taps, LANES), 0), iota((taps, LANES), 1)
    gather_own_ref[...] = (spot == (tap & (D1 - 1)) * (D2 * D3) + (tap >> 7)).astype(F32).astype(BF16)

    def gather_last(number, to_ref):
        hots = [
            hot_of(
                jnp.sum(
                    jnp.where(id_lane == k * shards * units + number, last_ids_ref[...], 0), axis=1, keepdims=True
                )
            )
            for k in range(BAG)
        ]
        to_ref[...] = dot(jnp.concatenate(hots, axis=0), last_by_d3_ref[...])

    def make_group(number, part, which, from_ref, diag_ref):
        base = number * unit + part * group
        for k in range(BAG):
            for q in range(group):
                at = dest_ref[k * queries + base + q]
                staged_ref[which, k, q] = left_ref[at]
        right = jnp.concatenate(
            [staged_ref[which, k].reshape(group * D1, wide) for k in range(BAG)], axis=1
        )
        pieces = [[None] * BAG for _ in range(D2 * D3)]
        for k in range(BAG):
            start = k * unit + part * group
            for tile in range(D3 // 2):
                both = from_ref[start : start + group, tile * LANES : (tile + 1) * LANES]
                low = jnp.where(low_half, both, 0.0)
                high = jnp.where(low_half, 0.0, both)
                pieces[2 * tile][k] = low
                pieces[D3 + 2 * tile][k] = pltpu.roll(low, rank, 1)
                pieces[2 * tile + 1][k] = pltpu.roll(high, rank, 1)
                pieces[D3 + 2 * tile + 1][k] = high
        lasts = jnp.concatenate([jnp.concatenate(p, axis=1) for p in pieces], axis=0).astype(BF16)
        product = dot_nt(lasts, right)
        for e in range(D2 * D3):
            at = e * group
            mine = jnp.concatenate(
                [product[at : at + 16, :LANES], product[at + 16 : at + 32, LANES:]], axis=0
            )
            diag_ref[part * group : (part + 1) * group, e * LANES : (e + 1) * LANES] = jnp.where(
                own, mine, 0.0
            ).astype(BF16)

    def make_unit(to, number, from_ref, diag_ref):
        for part in range(per_unit):
            make_group(to * units + number, part, number * per_unit + part, from_ref, diag_ref)
        out_ref[to, number * unit : (number + 1) * unit, :] = dot(
            diag_ref[...], gather_own_ref[...]
        ).astype(BF16)

    def send_of(i):
        to = lax.rem(me + 1 + i, shards)
        return pltpu.make_async_remote_copy(
            src_ref=out_ref.at[to],
            dst_ref=recv_ref.at[me],
            send_sem=pooled_send.at[i],
            recv_sem=pooled_recv.at[i],
            device_id={"tables": to},
            device_id_type=MESH,
        )

    gather_last(lax.rem(me + 1, shards) * units, last_a_ref)
    pl.semaphore_wait(barrier, shards + replicas - 2)

    def make_owner(i, carry):
        to, after = lax.rem(me + 1 + i, shards), lax.rem(me + 2 + i, shards)
        gather_last(to * units + 1, last_b_ref)
        make_unit(to, 0, last_a_ref, diag_a_ref)
        gather_last(after * units, last_a_ref)
        make_unit(to, 1, last_b_ref, diag_b_ref)

        @pl.when(i < shards - 1)
        def _():
            send_of(i).start()

        return carry

    lax.fori_loop(0, shards, make_owner, 0)
    fetches[2].start()
    recv_ref[me] = out_ref[me]
    for i in range(shards - 1):
        send_of(i).wait()
    fetches[0].wait()
    fetches[1].wait()

    first = jnp.concatenate([recv_ref[t] for t in range(shards)], axis=1).astype(F32)
    crossed = first
    for layer in range(down_v.shape[0]):
        low = dot(crossed.astype(BF16), down_v[layer]).astype(BF16)
        lifted = dot(low, up_v[layer])
        crossed = first * (lifted + bias_ref[layer : layer + 1, :].astype(F32)) + crossed
    mine_ref[...] = crossed.astype(BF16)
    pair = pltpu.make_async_remote_copy(
        src_ref=mine_ref, dst_ref=theirs_ref, send_sem=pair_send, recv_sem=pair_recv,
        device_id={"replica": sibling}, device_id_type=MESH,
    )
    pair.start()
    fetches[2].wait()

    def summed(rows_ref):
        sum_ref[...] = jnp.zeros_like(sum_ref)

        def step(t, carry):
            span = down_v.shape[1] // D1
            weight = jnp.concatenate(
                [left_ref[pl.ds((2 * t + h) * span, span)].reshape(span * D1, lanes) for h in range(2)], axis=1
            )
            hidden = dot(rows_ref[...], weight)
            for half in range(2):
                at = 2 * t + half
                unit = hidden[:, half * lanes : (half + 1) * lanes] + top_bias_ref[pl.ds(at, 1), :]
                unit = jnp.maximum(unit, 0.0).astype(BF16).astype(F32)
                sum_ref[:mine] += unit * out_weight_ref[pl.ds(at, 1), :]
            return carry

        lax.fori_loop(0, shards // 2, step, 0)
        return jnp.sum(jnp.transpose(sum_ref[...]), axis=0, keepdims=True)

    ours = summed(mine_ref)
    pair.wait()
    part_ref[...] = jnp.broadcast_to(summed(theirs_ref), part_ref.shape)
    back = pltpu.make_async_remote_copy(
        src_ref=part_ref, dst_ref=part_in_ref, send_sem=part_send, recv_sem=part_recv,
        device_id={"replica": sibling}, device_id_type=MESH,
    )
    back.start()
    back.wait()
    logits = (ours + part_in_ref[:1])[:, :mine] + prior_ref[...]
    both_ref[:1] = logits
    clicks = 1.0 / (1.0 + jnp.exp(-logits))
    click_ref[0] = jnp.broadcast_to(jnp.sum(clicks, axis=1, keepdims=True), click_ref.shape[1:])
    tells = []
    for i in range(1, replicas):
        tells.append(
            pltpu.make_async_remote_copy(
                src_ref=click_ref.at[0],
                dst_ref=click_ref.at[i],
                send_sem=click_send.at[i],
                recv_sem=click_recv.at[i],
                device_id={"replica": lax.rem(rep + i, replicas)},
                device_id_type=MESH,
            )
        )
    for tell in tells:
        tell.start()
    for tell in tells:
        tell.wait()
    total = click_ref[0]
    for i in range(1, replicas):
        total = total + click_ref[i]
    both_ref[1:] = (replicas * mine) * clicks / total[:1, :1]


def main(
    dest, owner, slot, last_ids, core_first, core_middle, core_last,
    weight, cross_down, cross_up, cross_bias, top_bias, out_weight, prior,
):
    items = dest.size
    groups, rank, wide = core_middle.shape
    slots = -(-(items + groups * TILE) // (2 * STEP)) * 2 * STEP
    shards, replicas = lax.axis_size("tables"), lax.axis_size("replica")
    queries = prior.shape[1]
    feat = cross_down.shape[1]
    padded = -(-queries // LANES) * LANES
    unit = last_ids.shape[0]
    smem = pl.BlockSpec(memory_space=pltpu.SMEM)
    vmem = pl.BlockSpec(memory_space=pltpu.VMEM)
    anywhere = pl.BlockSpec(memory_space=pl.ANY)
    dma = pltpu.SemaphoreType.DMA
    return pl.pallas_call(
        functools.partial(main_kernel, items),
        out_shape=jax.ShapeDtypeStruct((2, queries), F32),
        in_specs=[smem, smem, vmem, vmem, vmem, vmem, vmem, anywhere, anywhere, anywhere, vmem, vmem, vmem, vmem],
        out_specs=vmem,
        scratch_shapes=[
            pltpu.VMEM((groups, 2 * rank, 2 * wide), BF16),
            pltpu.VMEM(core_last.shape, BF16),
            pltpu.VMEM((slots, D1, wide), BF16),
            pltpu.VMEM((STEP // TILE, TILE * D1, wide), F32),
            pltpu.VMEM((STEP, core_first.shape[1]), BF16),
            pltpu.VMEM((STEP, core_first.shape[1]), BF16),
            pltpu.VMEM((BAG * unit, core_last.shape[1]), F32),
            pltpu.VMEM((BAG * unit, core_last.shape[1]), F32),
            pltpu.VMEM((queries // TILE, BAG, TILE, D1, wide), BF16),
            pltpu.VMEM((unit, D2 * D3 * LANES), BF16),
            pltpu.VMEM((unit, D2 * D3 * LANES), BF16),
            pltpu.VMEM((D2 * D3 * LANES, LANES), BF16),
            pltpu.VMEM((shards, queries, LANES), BF16),
            pltpu.VMEM((shards, queries, LANES), BF16),
            pltpu.VMEM((queries, feat), BF16),
            pltpu.VMEM((queries, feat), BF16),
            pltpu.VMEM(cross_down.shape, BF16),
            pltpu.VMEM(cross_up.shape, BF16),
            pltpu.VMEM((8, padded), F32),
            pltpu.VMEM((8, padded), F32),
            pltpu.VMEM((replicas, 8, LANES), F32),
            pltpu.VMEM((padded, LANES), F32),
            dma((shards,)),
            dma((shards,)),
            dma((3,)),
            dma,
            dma,
            dma,
            dma,
            dma((replicas,)),
            dma((replicas,)),
        ],
        compiler_params=pltpu.CompilerParams(
            collective_id=1, has_side_effects=True, vmem_limit_bytes=60 * 2**20
        ),
        cost_estimate=pl.CostEstimate(flops=int(100e9), bytes_accessed=24000000, transcendentals=0),
        name="main",
    )(
        dest.reshape(-1), owner, slot, last_ids, core_first, core_middle, core_last,
        weight.reshape(-1, D1, LANES), cross_down, cross_up, cross_bias, top_bias, out_weight, prior,
    )


def body(
    core_first,
    core_middle,
    core_last,
    idx_first,
    idx_middle,
    idx_last,
    bag_lengths,
    cross_down,
    cross_up,
    cross_bias,
    top_weight,
    top_bias,
    out_weight,
    prior,
):
    shards = lax.axis_size("tables")
    queries = idx_first.shape[2]

    core = lax.rem(lax.axis_index("replica"), 2)
    half = top_weight.shape[1] // 2
    part = lax.dynamic_slice_in_dim(top_weight, core * half, half, axis=1)
    weight = lax.all_gather(part, "tables", axis=0)

    def my_units(values):
        return lax.dynamic_index_in_dim(values.reshape(shards, 2, half), core, 1, keepdims=False)

    in_bag = jnp.arange(BAG, dtype=I32)[None, :, None] < bag_lengths[0, 0].T[:, None, :]

    def by_table(values):
        return jnp.transpose(values[0, 0], (1, 2, 0))

    sent = jnp.concatenate(
        [
            by_table(idx_first),
            by_table(idx_middle),
            jnp.where(in_bag, by_table(idx_last), -1),
        ],
        axis=1,
    )
    at_owner = lax.all_to_all(sent, "tables", split_axis=0, concat_axis=0, tiled=True)
    at_owner = jnp.transpose(at_owner, (1, 0, 2))
    first_ids, middle_ids, last_ids = (
        at_owner[BAG * i : BAG * (i + 1)].reshape(-1, LANES) for i in range(3)
    )
    dest, owner, slot = order(first_ids, middle_ids, core_middle.shape[1])
    unit = queries // 2
    both = main(
        dest,
        owner,
        slot,
        last_ids.reshape(-1, unit).T,
        core_first[0],
        core_middle[0],
        core_last[0],
        weight,
        cross_down,
        cross_up,
        cross_bias,
        my_units(top_bias).astype(F32),
        my_units(out_weight).astype(F32),
        prior[0],
    )
    return (both[:1][None], both[1:][None])


def solution(mesh):
    in_specs = (
        P("tables", None, None),
        P("tables", None, None, None),
        P("tables", None, None),
        P("replica", "tables", None, None, None),
        P("replica", "tables", None, None, None),
        P("replica", "tables", None, None, None),
        P("replica", "tables", None, None),
        P(),
        P(),
        P(),
        P(None, "tables"),
        P(),
        P(),
        P("replica", "tables", None),
    )
    out_specs = (P("replica", "tables", None), P("replica", "tables", None))
    return jax.shard_map(body, mesh=mesh, in_specs=in_specs, out_specs=out_specs, check_vma=False)
```

```python
import jax
import jax.numpy as jnp
from jax import lax
from jax.experimental import pallas as pl
from jax.experimental.pallas import tpu as pltpu
from jax.sharding import PartitionSpec as P

D1 = 8
D2 = 2
D3 = 8
BAG = 2
TILE = 32
LANES = 128
STEP = 512

BF16 = jnp.bfloat16
F32 = jnp.float32
I32 = jnp.int32
MESH = pl.DeviceIdType.MESH


def iota(shape, dim):
    return lax.broadcasted_iota(I32, shape, dim)


def dot(a, b):
    return jnp.dot(a, b, preferred_element_type=F32)


def dot_nt(a, b):
    return lax.dot_general(a, b, (((1,), (1,)), ((), ())), preferred_element_type=F32)


def group_items(groups, got_ref, dest_ref, owner_ref, slot_ref, rank_ref, sums_ref):
    sources, _, width = got_ref.shape
    group_row = iota((groups, width), 0)
    lane_row = iota((LANES, width), 0)
    before = (iota((width, width), 0) < iota((width, width), 1)).astype(F32).astype(BF16)
    together = 8
    steps = BAG * sources // together
    per_bag = sources // together

    def rows_of(step, field):
        rows = []
        for u in range(together):
            source = lax.rem(step, per_bag) * together + u
            at = field * BAG + lax.div(step, per_bag)
            rows.append(got_ref[source, pl.ds(at, 1), :])
        return rows

    def count(step, seen):
        hots = [group_row == row for row in rows_of(step, 1)]
        ones = jnp.concatenate([h.astype(F32) for h in hots], axis=0)
        ranks = dot(ones.astype(BF16), before)
        sizes = jnp.sum(ones, axis=1, keepdims=True)
        rows = []
        for u in range(together):
            at = slice(u * groups, (u + 1) * groups)
            rows.append(jnp.sum(jnp.where(hots[u], ranks[at] + seen, 0.0), axis=0, keepdims=True))
            seen = seen + sizes[at]
        rank_ref[pl.ds(pl.multiple_of(step * together, together), together), :] = jnp.concatenate(rows, axis=0)
        return seen

    counts = lax.fori_loop(0, steps, count, jnp.zeros((groups, 1), F32))
    tiles = jnp.floor((counts + (TILE - 1)) * (1.0 / TILE))
    tiles = jnp.broadcast_to(tiles, (groups, LANES))
    high = jnp.floor(tiles * (1.0 / 16))
    low = tiles - 16.0 * high
    above = (iota((groups, groups), 0) > iota((groups, groups), 1)).astype(F32).astype(BF16)
    offset = 16.0 * dot(above, high.astype(BF16)) + dot(above, low.astype(BF16))
    offset = offset[:, :1]
    tile_lane = iota((groups, owner_ref.shape[1]), 1)
    owner_ref[...] = jnp.broadcast_to(
        jnp.sum((offset.astype(I32) <= tile_lane).astype(I32), axis=0, keepdims=True) - 1, owner_ref.shape
    )
    sums_ref[...] = jnp.zeros_like(sums_ref)

    def place(step, carry):
        first = pl.multiple_of(step * together, together)
        middles = rows_of(step, 1)
        starts = [jnp.sum(jnp.where(group_row == row, offset, 0.0), axis=0, keepdims=True) for row in middles]
        dests = (rank_ref[pl.ds(first, together), :] + TILE * jnp.concatenate(starts, axis=0)).astype(I32)
        dests = jnp.where(jnp.concatenate(middles, axis=0) < 0, -1, dests)
        dest_ref[pl.ds(first, together), :] = dests
        ids = jnp.concatenate(rows_of(step, 0), axis=0)
        lanes, highs, lows, rows = dests & (LANES - 1), (ids >> 4).astype(F32), (ids & 15).astype(F32), dests >> 7
        values, spots = [], []
        for u in range(together):
            at = slice(u, u + 1)
            at_lane = lane_row == lanes[at]
            values.append(
                jnp.concatenate(
                    [jnp.where(at_lane, highs[at], 0.0), jnp.where(at_lane, lows[at], 0.0)], axis=0
                ).astype(BF16)
            )
            spots.append((lane_row == rows[at]).astype(F32).astype(BF16))
        sums_ref[...] += dot_nt(jnp.concatenate(values, axis=1), jnp.concatenate(spots, axis=1))
        return carry

    lax.fori_loop(0, steps, place, 0)
    slot_ref[...] = (16.0 * sums_ref[:LANES, :] + sums_ref[LANES:, :]).astype(I32)


def main_kernel(
    idx_first_ref, idx_middle_ref, idx_last_ref, lengths_ref, first_ref, middle_ref, last_ref,
    top_ref, down_ref, up_ref, bias_ref, units_ref, prior_ref,
    both_ref, weight_ref,
    sent_ref, got_ref, last_ids_ref, dest_v, owner_v, slot_ref, rank_ref, places_ref, dest_ref, owner_ref,
    pair_ref, last_by_d3_ref, left_ref, spread_ref, cores_a_ref, cores_b_ref, last_a_ref, last_b_ref,
    staged_ref, diag_a_ref, diag_b_ref, gather_own_ref,
    out_ref, recv_ref, mine_ref, theirs_ref, down_v, up_v, part_ref, part_in_ref, click_ref, sum_ref,
    ids_send, ids_recv, spread_send, spread_recv, forward_send, forward_recv, local_sem,
    pooled_send, pooled_recv, weight_sem, pair_send, pair_recv, part_send, part_recv,
    click_send, click_recv,
):
    shards, mine, lanes = recv_ref.shape
    replicas = lax.axis_size("replica")
    me, rep = lax.axis_index("tables"), lax.axis_index("replica")
    sibling = rep + 1 - 2 * lax.rem(rep, 2)
    barrier = pltpu.get_barrier_semaphore()
    for i in range(1, shards):
        pl.semaphore_signal(
            barrier, inc=1, device_id={"tables": lax.rem(me + i, shards)}, device_id_type=MESH
        )
    for i in range(1, replicas):
        pl.semaphore_signal(
            barrier, inc=1, device_id={"replica": lax.rem(rep + i, replicas)}, device_id_type=MESH
        )
    core = lax.rem(rep, 2)
    groups, rank, wide = middle_ref.shape
    rows = first_ref.shape[0]
    side = 4 if shards == 16 else 1
    row, column = lax.div(me, side), lax.rem(me, side)
    span = down_v.shape[1] // D1
    fetches = [
        pltpu.make_async_copy(down_ref, down_v, weight_sem.at[0]),
        pltpu.make_async_copy(up_ref, up_v, weight_sem.at[1]),
        pltpu.make_async_copy(weight_ref, left_ref.at[pl.ds(0, weight_ref.shape[0])], weight_sem.at[2]),
    ]
    fetches[0].start()
    fetches[1].start()

    own_weight = top_ref.at[:, :, pl.ds(pl.multiple_of(core * lanes, lanes), lanes)]
    half = span // 2

    def shard_part(shard, part):
        return weight_ref.at[pl.ds(shard * span + part * half, half)]

    keep = pltpu.make_async_copy(own_weight, weight_ref.at[pl.ds(me * span, span)], local_sem)
    keep.start()

    def spread_of(part, away):
        to = row * side + lax.rem(column + away, side) if part == 0 else lax.rem(row + away, side) * side + column
        return pltpu.make_async_remote_copy(
            src_ref=shard_part(me, part), dst_ref=shard_part(me, part),
            send_sem=spread_send.at[part, away], recv_sem=spread_recv.at[part, away],
            device_id={"tables": to}, device_id_type=MESH,
        )

    def forward_of(part, away, other):
        if part == 0:
            shard = row * side + lax.rem(column + other, side)
            to = lax.rem(row + away, side) * side + column
        else:
            shard = lax.rem(row + other, side) * side + column
            to = row * side + lax.rem(column + away, side)
        return pltpu.make_async_remote_copy(
            src_ref=shard_part(shard, part), dst_ref=shard_part(shard, part),
            send_sem=forward_send.at[part, away, other], recv_sem=forward_recv.at[part, away, other],
            device_id={"tables": to}, device_id_type=MESH,
        )

    spreads = [spread_of(part, away) for away in range(1, side) for part in range(2)]
    forwards = [
        forward_of(part, away, other)
        for other in range(side)
        for away in range(1, side)
        for part in range(2)
    ]

    sent_ref[...] = jnp.full_like(sent_ref, -1)
    for t in range(shards):
        in_bag = iota((BAG, mine), 0) < lengths_ref[t : t + 1, :]
        sent_ref[t, 0:BAG, :mine] = idx_first_ref[t]
        sent_ref[t, BAG : 2 * BAG, :mine] = idx_middle_ref[t]
        sent_ref[t, 2 * BAG : 3 * BAG, :mine] = jnp.where(in_bag, idx_last_ref[t], -1)

    def ids_of(i):
        to = lax.rem(me + i, shards)
        return pltpu.make_async_remote_copy(
            src_ref=sent_ref.at[to], dst_ref=got_ref.at[me],
            send_sem=ids_send.at[i], recv_sem=ids_recv.at[i],
            device_id={"tables": to}, device_id_type=MESH,
        )

    pl.semaphore_wait(barrier, shards + replicas - 2)
    for i in range(1, shards):
        ids_of(i).start()
    keep.wait()
    for spread in spreads:
        spread.start()
    got_ref[me] = sent_ref[me]

    def make_pair(g, carry):
        core = middle_ref[pl.ds(g, 1)].reshape(rank, wide)
        zero = jnp.zeros_like(core)
        pair_ref[pl.ds(g, 1), :rank, :wide] = core.reshape(1, rank, wide)
        pair_ref[pl.ds(g, 1), :rank, wide:] = zero.reshape(1, rank, wide)
        pair_ref[pl.ds(g, 1), rank:, :wide] = zero.reshape(1, rank, wide)
        pair_ref[pl.ds(g, 1), rank:, wide:] = core.reshape(1, rank, wide)
        return carry

    lax.fori_loop(0, groups, make_pair, 0)
    width = last_ref.shape[1]
    from_row, to_lane = iota((width, width), 0), iota((width, width), 1)
    swap = (to_lane == (from_row & (D3 - 1)) * rank + (from_row >> 3)).astype(F32).astype(BF16)
    last_by_d3_ref[...] = dot(last_ref[...], swap).astype(BF16)

    taps = D2 * D3 * LANES
    tap, spot = iota((taps, LANES), 0), iota((taps, LANES), 1)
    gather_own_ref[...] = (spot == (tap & (D1 - 1)) * (D2 * D3) + (tap >> 7)).astype(F32).astype(BF16)

    for i in range(1, shards):
        ids_of(i).wait()
    group_items(groups, got_ref, dest_v, owner_v, slot_ref, rank_ref, places_ref)
    to_scalars = [
        pltpu.make_async_copy(dest_v, dest_ref, weight_sem.at[3]),
        pltpu.make_async_copy(owner_v, owner_ref, weight_sem.at[4]),
    ]
    for copy in to_scalars:
        copy.start()
    last_ids_ref[...] = jnp.transpose(
        got_ref[...].reshape(shards * got_ref.shape[1], got_ref.shape[2]).astype(F32)
    )
    for spread in spreads:
        spread.wait()
    for forward in forwards:
        forward.start()
    for copy in to_scalars:
        copy.wait()

    per_step = STEP // TILE
    pairs = left_ref.shape[0] // (2 * STEP)
    slot_lane = iota((LANES, LANES), 1)

    def hot_of(ids):
        return (iota((ids.shape[0], rows), 1) == ids).astype(F32).astype(BF16)

    def gather_first(step, to_ref):
        hots = []
        for c in range(STEP // LANES):
            column = step * (STEP // LANES) + c
            hots.append(
                hot_of(jnp.sum(jnp.where(slot_lane == column, slot_ref[...], 0), axis=1, keepdims=True))
            )
        to_ref[...] = dot(jnp.concatenate(hots, axis=0), first_ref[...]).astype(BF16)

    def make_left(step, from_ref):
        for t in range(per_step):
            owner = jnp.clip(owner_ref[0, step * per_step + t], 0, groups - 1)
            stacked = jnp.concatenate(
                [
                    from_ref[t * TILE : (t + 1) * TILE, p * LANES : (p + 1) * LANES]
                    for p in range(D1 // 2)
                ],
                axis=0,
            )
            pair = pair_ref[pl.ds(owner, 1)].reshape(2 * rank, 2 * wide)
            product = dot(stacked, pair)
            for p in range(D1 // 2):
                for half in range(2):
                    for s in range(TILE // 8):
                        spread_ref[t, pl.ds(s * 64 + 2 * p + half, 8, stride=D1), :] = product[
                            p * TILE + s * 8 : p * TILE + s * 8 + 8, half * wide : (half + 1) * wide
                        ]
            left_ref[pl.ds((step * per_step + t) * TILE, TILE)] = (
                spread_ref[t].reshape(TILE, D1, wide).astype(BF16)
            )

    gather_first(0, cores_a_ref)

    def left_pair(pair, carry):
        gather_first(2 * pair + 1, cores_b_ref)
        make_left(2 * pair, cores_a_ref)
        gather_first(2 * pair + 2, cores_a_ref)
        make_left(2 * pair + 1, cores_b_ref)
        return carry

    lax.fori_loop(0, pairs, left_pair, 0)

    group = TILE
    unit = diag_a_ref.shape[0]
    units = mine // unit
    per_unit = unit // group
    id_lane = iota((unit, LANES), 1)
    low_half = iota((group, LANES), 1) < rank
    own = (iota((group, LANES), 1) >> 3) == (iota((group, LANES), 0) & 15)
    def gather_last(source, number, to_ref):
        rows_here = last_ids_ref[number * unit : (number + 1) * unit, :]
        hots = []
        for k in range(BAG):
            mark = source * got_ref.shape[1] + 2 * BAG + k
            ids = jnp.sum(jnp.where(id_lane == mark, rows_here, 0.0), axis=1, keepdims=True)
            hots.append(hot_of(ids.astype(I32)))
        to_ref[...] = dot(jnp.concatenate(hots, axis=0), last_by_d3_ref[...])

    def make_group(source, number, part, from_ref, diag_ref):
        base = number * unit + part * group
        which = number * per_unit + part
        for k in range(BAG):
            for q in range(group):
                at = jnp.clip(dest_ref[k * shards + source, base + q], 0, left_ref.shape[0] - 1)
                staged_ref[which, k, q] = left_ref[at]
        right = jnp.concatenate(
            [staged_ref[which, k].reshape(group * D1, wide) for k in range(BAG)], axis=1
        )
        pieces = [[None] * BAG for _ in range(D2 * D3)]
        for k in range(BAG):
            start = k * unit + part * group
            for tile in range(D3 // 2):
                both = from_ref[start : start + group, tile * LANES : (tile + 1) * LANES]
                low = jnp.where(low_half, both, 0.0)
                high = jnp.where(low_half, 0.0, both)
                pieces[2 * tile][k] = low
                pieces[D3 + 2 * tile][k] = pltpu.roll(low, rank, 1)
                pieces[2 * tile + 1][k] = pltpu.roll(high, rank, 1)
                pieces[D3 + 2 * tile + 1][k] = high
        lasts = jnp.concatenate([jnp.concatenate(p, axis=1) for p in pieces], axis=0).astype(BF16)
        product = dot_nt(lasts, right)
        for e in range(D2 * D3):
            at = e * group
            mine = jnp.concatenate(
                [product[at : at + 16, :LANES], product[at + 16 : at + 32, LANES:]], axis=0
            )
            diag_ref[part * group : (part + 1) * group, e * LANES : (e + 1) * LANES] = jnp.where(
                own, mine, 0.0
            ).astype(BF16)

    def make_unit(to, number, from_ref, diag_ref):
        for part in range(per_unit):
            make_group(to, number, part, from_ref, diag_ref)
        out_ref[to, number * unit : (number + 1) * unit, :] = dot(
            diag_ref[...], gather_own_ref[...]
        ).astype(BF16)

    def send_of(i):
        to = lax.rem(me + 1 + i, shards)
        return pltpu.make_async_remote_copy(
            src_ref=out_ref.at[to],
            dst_ref=recv_ref.at[me],
            send_sem=pooled_send.at[i],
            recv_sem=pooled_recv.at[i],
            device_id={"tables": to},
            device_id_type=MESH,
        )

    gather_last(lax.rem(me + 1, shards), 0, last_a_ref)

    def make_owner(i, carry):
        to, after = lax.rem(me + 1 + i, shards), lax.rem(me + 2 + i, shards)
        gather_last(to, 1, last_b_ref)
        make_unit(to, 0, last_a_ref, diag_a_ref)
        gather_last(after, 0, last_a_ref)
        make_unit(to, 1, last_b_ref, diag_b_ref)

        @pl.when(i < shards - 1)
        def _():
            send_of(i).start()

        return carry

    lax.fori_loop(0, shards, make_owner, 0)
    for forward in forwards:
        forward.wait()
    fetches[2].start()
    recv_ref[me] = out_ref[me]
    for i in range(shards - 1):
        send_of(i).wait()
    fetches[0].wait()
    fetches[1].wait()

    first = jnp.concatenate([recv_ref[t] for t in range(shards)], axis=1).astype(F32)
    crossed = first
    for layer in range(down_v.shape[0]):
        low = dot(crossed.astype(BF16), down_v[layer]).astype(BF16)
        lifted = dot(low, up_v[layer])
        crossed = first * (lifted + bias_ref[layer : layer + 1, :].astype(F32)) + crossed
    mine_ref[...] = crossed.astype(BF16)
    pair = pltpu.make_async_remote_copy(
        src_ref=mine_ref, dst_ref=theirs_ref, send_sem=pair_send, recv_sem=pair_recv,
        device_id={"replica": sibling}, device_id_type=MESH,
    )
    pair.start()
    fetches[2].wait()

    def summed(rows_ref):
        sum_ref[...] = jnp.zeros_like(sum_ref)

        def step(t, carry):
            weight = jnp.concatenate(
                [left_ref[pl.ds((2 * t + h) * span, span)].reshape(span * D1, lanes) for h in range(2)], axis=1
            )
            hidden = dot(rows_ref[...], weight)
            for half in range(2):
                at = 2 * t + half
                unit = hidden[:, half * lanes : (half + 1) * lanes] + units_ref[pl.ds(2 * at + core, 1), :]
                unit = jnp.maximum(unit, 0.0).astype(BF16).astype(F32)
                sum_ref[:mine] += unit * units_ref[pl.ds(2 * (shards + at) + core, 1), :]
            return carry

        lax.fori_loop(0, shards // 2, step, 0)
        return jnp.sum(jnp.transpose(sum_ref[...]), axis=0, keepdims=True)

    ours = summed(mine_ref)
    pair.wait()
    part_ref[...] = jnp.broadcast_to(summed(theirs_ref), part_ref.shape)
    back = pltpu.make_async_remote_copy(
        src_ref=part_ref, dst_ref=part_in_ref, send_sem=part_send, recv_sem=part_recv,
        device_id={"replica": sibling}, device_id_type=MESH,
    )
    back.start()
    back.wait()
    logits = (ours + part_in_ref[:1])[:, :mine] + prior_ref[...]
    both_ref[:1] = logits
    clicks = 1.0 / (1.0 + jnp.exp(-logits))
    click_ref[0] = jnp.broadcast_to(jnp.sum(clicks, axis=1, keepdims=True), click_ref.shape[1:])
    tells = []
    for i in range(1, replicas):
        tells.append(
            pltpu.make_async_remote_copy(
                src_ref=click_ref.at[0],
                dst_ref=click_ref.at[i],
                send_sem=click_send.at[i],
                recv_sem=click_recv.at[i],
                device_id={"replica": lax.rem(rep + i, replicas)},
                device_id_type=MESH,
            )
        )
    for tell in tells:
        tell.start()
    for tell in tells:
        tell.wait()
    total = click_ref[0]
    for i in range(1, replicas):
        total = total + click_ref[i]
    both_ref[1:] = (replicas * mine) * clicks / total[:1, :1]


def main(
    idx_first, idx_middle, idx_last, lengths, core_first, core_middle, core_last,
    top_weight, cross_down, cross_up, cross_bias, units, prior,
):
    groups, rank, wide = core_middle.shape
    shards, replicas = lax.axis_size("tables"), lax.axis_size("replica")
    queries = prior.shape[1]
    items = shards * queries * BAG
    slots = -(-(items + groups * TILE) // (2 * STEP)) * 2 * STEP
    feat, hid = top_weight.shape
    padded = -(-queries // LANES) * LANES
    unit = queries // 2
    owners = -(-(slots // TILE) // LANES) * LANES
    side = 4 if shards == 16 else 1
    vmem = pl.BlockSpec(memory_space=pltpu.VMEM)
    anywhere = pl.BlockSpec(memory_space=pl.ANY)
    dma = pltpu.SemaphoreType.DMA
    return pl.pallas_call(
        main_kernel,
        out_shape=(
            jax.ShapeDtypeStruct((2, queries), F32),
            jax.ShapeDtypeStruct((shards * feat // D1, D1, LANES), BF16),
        ),
        in_specs=[vmem] * 7 + [anywhere] * 3 + [vmem] * 3,
        out_specs=(vmem, anywhere),
        scratch_shapes=[
            pltpu.VMEM((shards, 8, padded), I32),
            pltpu.VMEM((shards, 8, padded), I32),
            pltpu.VMEM((padded, shards * 8), F32),
            pltpu.VMEM((BAG * shards, padded), I32),
            pltpu.VMEM((8, owners), I32),
            pltpu.VMEM((LANES, LANES), I32),
            pltpu.VMEM((BAG * shards, padded), F32),
            pltpu.VMEM((2 * LANES, LANES), F32),
            pltpu.SMEM((BAG * shards, padded), I32),
            pltpu.SMEM((8, owners), I32),
            pltpu.VMEM((groups, 2 * rank, 2 * wide), BF16),
            pltpu.VMEM(core_last.shape, BF16),
            pltpu.VMEM((slots, D1, wide), BF16),
            pltpu.VMEM((STEP // TILE, TILE * D1, wide), F32),
            pltpu.VMEM((STEP, core_first.shape[1]), BF16),
            pltpu.VMEM((STEP, core_first.shape[1]), BF16),
            pltpu.VMEM((BAG * unit, core_last.shape[1]), F32),
            pltpu.VMEM((BAG * unit, core_last.shape[1]), F32),
            pltpu.VMEM((queries // TILE, BAG, TILE, D1, wide), BF16),
            pltpu.VMEM((unit, D2 * D3 * LANES), BF16),
            pltpu.VMEM((unit, D2 * D3 * LANES), BF16),
            pltpu.VMEM((D2 * D3 * LANES, LANES), BF16),
            pltpu.VMEM((shards, queries, LANES), BF16),
            pltpu.VMEM((shards, queries, LANES), BF16),
            pltpu.VMEM((queries, feat), BF16),
            pltpu.VMEM((queries, feat), BF16),
            pltpu.VMEM(cross_down.shape, BF16),
            pltpu.VMEM(cross_up.shape, BF16),
            pltpu.VMEM((8, padded), F32),
            pltpu.VMEM((8, padded), F32),
            pltpu.VMEM((replicas, 8, LANES), F32),
            pltpu.VMEM((padded, LANES), F32),
            dma((shards,)),
            dma((shards,)),
            dma((2, side)),
            dma((2, side)),
            dma((2, side, side)),
            dma((2, side, side)),
            dma,
            dma((shards,)),
            dma((shards,)),
            dma((5,)),
            dma,
            dma,
            dma,
            dma,
            dma((replicas,)),
            dma((replicas,)),
        ],
        compiler_params=pltpu.CompilerParams(
            collective_id=1, has_side_effects=True, vmem_limit_bytes=60 * 2**20
        ),
        cost_estimate=pl.CostEstimate(flops=int(100e9), bytes_accessed=24000000, transcendentals=0),
        name="main",
    )(
        idx_first, idx_middle, idx_last, lengths, core_first, core_middle, core_last,
        top_weight.reshape(feat // D1, D1, hid), cross_down, cross_up, cross_bias, units, prior,
    )


def body(
    core_first,
    core_middle,
    core_last,
    idx_first,
    idx_middle,
    idx_last,
    bag_lengths,
    cross_down,
    cross_up,
    cross_bias,
    top_weight,
    top_bias,
    out_weight,
    prior,
):
    def by_table(values):
        return jnp.transpose(values[0, 0], (1, 2, 0))

    units = jnp.concatenate([top_bias, out_weight]).astype(F32).reshape(-1, LANES)
    both, _ = main(
        by_table(idx_first),
        by_table(idx_middle),
        by_table(idx_last),
        bag_lengths[0, 0].T,
        core_first[0],
        core_middle[0],
        core_last[0],
        top_weight,
        cross_down,
        cross_up,
        cross_bias,
        units,
        prior[0],
    )
    return (both[:1][None], both[1:][None])


def solution(mesh):
    in_specs = (
        P("tables", None, None),
        P("tables", None, None, None),
        P("tables", None, None),
        P("replica", "tables", None, None, None),
        P("replica", "tables", None, None, None),
        P("replica", "tables", None, None, None),
        P("replica", "tables", None, None),
        P(),
        P(),
        P(),
        P(None, "tables"),
        P(),
        P(),
        P("replica", "tables", None),
    )
    out_specs = (P("replica", "tables", None), P("replica", "tables", None))
    return jax.shard_map(body, mesh=mesh, in_specs=in_specs, out_specs=out_specs, check_vma=False)
```

```python
import jax
import jax.numpy as jnp
from jax import lax
from jax.experimental import pallas as pl
from jax.experimental.pallas import tpu as pltpu
from jax.sharding import PartitionSpec as P

D1 = 8
D2 = 2
D3 = 8
BAG = 2
TILE = 32
LANES = 128
STEP = 512

BF16 = jnp.bfloat16
F32 = jnp.float32
I32 = jnp.int32
MESH = pl.DeviceIdType.MESH


def iota(shape, dim):
    return lax.broadcasted_iota(I32, shape, dim)


def dot(a, b):
    return jnp.dot(a, b, preferred_element_type=F32)


def dot_nt(a, b):
    return lax.dot_general(a, b, (((1,), (1,)), ((), ())), preferred_element_type=F32)


def group_items(groups, slots, got_ref, dest_ref, owner_ref, slot_ref, rank_ref, sums_ref):
    sources, _, width = got_ref.shape
    group_row = iota((groups, width), 0)
    lane_row = iota((LANES, width), 0)
    before = (iota((width, width), 0) < iota((width, width), 1)).astype(F32).astype(BF16)
    together = 8
    steps = BAG * sources // together
    per_bag = sources // together

    def rows_of(step, field):
        rows = []
        for u in range(together):
            source = lax.rem(step, per_bag) * together + u
            at = field * BAG + lax.div(step, per_bag)
            rows.append(got_ref[source, pl.ds(at, 1), :])
        return rows

    def count(step, seen):
        hots = [group_row == row for row in rows_of(step, 1)]
        ones = jnp.concatenate([h.astype(F32) for h in hots], axis=0)
        ranks = dot(ones.astype(BF16), before)
        sizes = jnp.sum(ones, axis=1, keepdims=True)
        rows = []
        for u in range(together):
            at = slice(u * groups, (u + 1) * groups)
            rows.append(jnp.sum(jnp.where(hots[u], ranks[at] + seen, 0.0), axis=0, keepdims=True))
            seen = seen + sizes[at]
        rank_ref[pl.ds(pl.multiple_of(step * together, together), together), :] = jnp.concatenate(rows, axis=0)
        return seen

    counts = lax.fori_loop(0, steps, count, jnp.zeros((groups, 1), F32))
    tiles = jnp.floor((counts + (TILE - 1)) * (1.0 / TILE))
    tiles = jnp.broadcast_to(tiles, (groups, LANES))
    high = jnp.floor(tiles * (1.0 / 16))
    low = tiles - 16.0 * high
    above = (iota((groups, groups), 0) > iota((groups, groups), 1)).astype(F32).astype(BF16)
    offset = 16.0 * dot(above, high.astype(BF16)) + dot(above, low.astype(BF16))
    offset = offset[:, :1]
    tile_lane = iota((groups, owner_ref.shape[1]), 1)
    reached = jnp.sum((offset.astype(I32) <= tile_lane).astype(I32), axis=0, keepdims=True)
    owner_ref[...] = jnp.broadcast_to(jnp.clip(reached - 1, 0, groups - 1), owner_ref.shape)
    sums_ref[...] = jnp.zeros_like(sums_ref)

    def place(step, carry):
        first = pl.multiple_of(step * together, together)
        middles = rows_of(step, 1)
        starts = [jnp.sum(jnp.where(group_row == row, offset, 0.0), axis=0, keepdims=True) for row in middles]
        dests = (rank_ref[pl.ds(first, together), :] + TILE * jnp.concatenate(starts, axis=0)).astype(I32)
        dests = jnp.where(jnp.concatenate(middles, axis=0) < 0, -1, dests)
        dest_ref[pl.ds(first, together), :] = jnp.clip(dests, 0, slots - 1)
        ids = jnp.concatenate(rows_of(step, 0), axis=0)
        lanes, highs, lows, rows = dests & (LANES - 1), (ids >> 4).astype(F32), (ids & 15).astype(F32), dests >> 7
        values, spots = [], []
        for u in range(together):
            at = slice(u, u + 1)
            at_lane = lane_row == lanes[at]
            values.append(
                jnp.concatenate(
                    [jnp.where(at_lane, highs[at], 0.0), jnp.where(at_lane, lows[at], 0.0)], axis=0
                ).astype(BF16)
            )
            spots.append((lane_row == rows[at]).astype(F32).astype(BF16))
        sums_ref[...] += dot_nt(jnp.concatenate(values, axis=1), jnp.concatenate(spots, axis=1))
        return carry

    lax.fori_loop(0, steps, place, 0)
    slot_ref[...] = (16.0 * sums_ref[:LANES, :] + sums_ref[LANES:, :]).astype(I32)


def main_kernel(
    idx_first_ref, idx_middle_ref, idx_last_ref, lengths_ref, first_ref, middle_ref, last_ref,
    top_ref, down_ref, up_ref, bias_ref, units_ref, prior_ref,
    both_ref, weight_ref,
    sent_ref, got_ref, last_ids_ref, dest_v, owner_v, slot_ref, rank_ref, places_ref, dest_ref, owner_ref,
    pair_ref, last_by_d3_ref, left_ref, spread_ref, cores_a_ref, cores_b_ref, last_a_ref, last_b_ref,
    staged_ref, diag_a_ref, diag_b_ref, gather_own_ref,
    out_ref, recv_ref, mine_ref, theirs_ref, down_v, up_v, part_ref, part_in_ref, click_ref, sum_ref,
    ids_send, ids_recv, spread_send, spread_recv, forward_send, forward_recv, local_sem,
    pooled_send, pooled_recv, weight_sem, pair_send, pair_recv, part_send, part_recv,
    click_send, click_recv,
):
    shards, mine, lanes = recv_ref.shape
    replicas = lax.axis_size("replica")
    me, rep = lax.axis_index("tables"), lax.axis_index("replica")
    sibling = rep + 1 - 2 * lax.rem(rep, 2)
    barrier = pltpu.get_barrier_semaphore()
    for i in range(1, shards):
        pl.semaphore_signal(
            barrier, inc=1, device_id={"tables": lax.rem(me + i, shards)}, device_id_type=MESH
        )
    for i in range(1, replicas):
        pl.semaphore_signal(
            barrier, inc=1, device_id={"replica": lax.rem(rep + i, replicas)}, device_id_type=MESH
        )
    core = lax.rem(rep, 2)
    groups, rank, wide = middle_ref.shape
    rows = first_ref.shape[0]
    side = 4 if shards == 16 else 1
    row, column = lax.div(me, side), lax.rem(me, side)
    span = down_v.shape[1] // D1
    fetches = [
        pltpu.make_async_copy(down_ref, down_v, weight_sem.at[0]),
        pltpu.make_async_copy(up_ref, up_v, weight_sem.at[1]),
        pltpu.make_async_copy(weight_ref, left_ref.at[pl.ds(0, weight_ref.shape[0])], weight_sem.at[2]),
    ]
    fetches[0].start()
    fetches[1].start()

    rows_of_part = span // 2
    keep = pltpu.make_async_copy(
        top_ref.at[:, :, pl.ds(pl.multiple_of(core * lanes, lanes), lanes)],
        weight_ref.at[pl.ds(me * span, span)],
        local_sem,
    )
    keep.start()

    def place_of(part, along, across):
        u, v = (column, row) if part == 0 else (row, column)
        u, v = lax.rem(u + along + side, side), lax.rem(v + across + side, side)
        return v * side + u if part == 0 else u * side + v

    def hop(part, shard, to, piece, mine_too, sems, at):
        start, count = part * rows_of_part, rows_of_part
        if piece is not None:
            count = rows_of_part // 2
            start = start + piece * count
        dst = weight_ref.at[pl.ds(shard * span + start, count)]
        src = dst
        if mine_too:
            src = top_ref.at[pl.ds(start, count), :, pl.ds(pl.multiple_of(core * lanes, lanes), lanes)]
        return pltpu.make_async_remote_copy(
            src_ref=src, dst_ref=dst, send_sem=sems[0].at[at], recv_sem=sems[1].at[at],
            device_id={"tables": to}, device_id_type=MESH,
        )

    ways = [(part, way, 1 - 2 * way) for part in range(2) for way in range(2)]

    def spread():
        return [
            hop(p, me, place_of(p, d, 0), None, True, (spread_send, spread_recv), (p, w, 0)) for p, w, d in ways
        ]

    def spread_on():
        return [
            hop(p, place_of(p, -d, 0), place_of(p, d, 0), w, False, (spread_send, spread_recv), (p, w, 1))
            for p, w, d in ways
        ]

    def forward(others):
        return [
            hop(
                p, place_of(p, j, 0), place_of(p, 0, d), None, j == 0, (forward_send, forward_recv), (p, w, 0, j)
            )
            for j in others
            for p, w, d in ways
        ]

    def forward_on(others):
        return [
            hop(
                p, place_of(p, j, -d), place_of(p, 0, d), w, False, (forward_send, forward_recv), (p, w, 1, j)
            )
            for j in others
            for p, w, d in ways
        ]

    def start(copies):
        for copy in copies:
            copy.start()

    def wait(copies):
        for copy in copies:
            copy.wait()

    sent_ref[...] = jnp.full_like(sent_ref, -1)
    for t in range(shards):
        in_bag = iota((BAG, mine), 0) < lengths_ref[t : t + 1, :]
        sent_ref[t, 0:BAG, :mine] = idx_first_ref[t]
        sent_ref[t, BAG : 2 * BAG, :mine] = idx_middle_ref[t]
        sent_ref[t, 2 * BAG : 3 * BAG, :mine] = jnp.where(in_bag, idx_last_ref[t], -1)

    def ids_of(i):
        to = lax.rem(me + i, shards)
        return pltpu.make_async_remote_copy(
            src_ref=sent_ref.at[to], dst_ref=got_ref.at[me],
            send_sem=ids_send.at[i], recv_sem=ids_recv.at[i],
            device_id={"tables": to}, device_id_type=MESH,
        )

    pl.semaphore_wait(barrier, shards + replicas - 2)
    for i in range(1, shards):
        ids_of(i).start()
    start(spread())
    start(forward([0]))
    got_ref[me] = sent_ref[me]

    def make_pair(g, carry):
        core = middle_ref[pl.ds(g, 1)].reshape(rank, wide)
        zero = jnp.zeros_like(core)
        pair_ref[pl.ds(g, 1), :rank, :wide] = core.reshape(1, rank, wide)
        pair_ref[pl.ds(g, 1), :rank, wide:] = zero.reshape(1, rank, wide)
        pair_ref[pl.ds(g, 1), rank:, :wide] = zero.reshape(1, rank, wide)
        pair_ref[pl.ds(g, 1), rank:, wide:] = core.reshape(1, rank, wide)
        return carry

    lax.fori_loop(0, groups, make_pair, 0)
    width = last_ref.shape[1]
    from_row, to_lane = iota((width, width), 0), iota((width, width), 1)
    swap = (to_lane == (from_row & (D3 - 1)) * rank + (from_row >> 3)).astype(F32).astype(BF16)
    last_by_d3_ref[...] = dot(last_ref[...], swap).astype(BF16)

    taps = D2 * D3 * LANES
    tap, spot = iota((taps, LANES), 0), iota((taps, LANES), 1)
    gather_own_ref[...] = (spot == (tap & (D1 - 1)) * (D2 * D3) + (tap >> 7)).astype(F32).astype(BF16)

    for i in range(1, shards):
        ids_of(i).wait()
    group_items(groups, left_ref.shape[0], got_ref, dest_v, owner_v, slot_ref, rank_ref, places_ref)
    to_scalars = [
        pltpu.make_async_copy(dest_v, dest_ref, weight_sem.at[3]),
        pltpu.make_async_copy(owner_v, owner_ref, weight_sem.at[4]),
    ]
    for copy in to_scalars:
        copy.start()
    last_ids_ref[...] = jnp.transpose(
        got_ref[...].reshape(shards * got_ref.shape[1], got_ref.shape[2]).astype(F32)
    )
    wait(spread())
    start(spread_on())
    start(forward([1, 3]))
    wait(forward([0]))
    start(forward_on([0]))
    for copy in to_scalars:
        copy.wait()

    per_step = STEP // TILE
    pairs = left_ref.shape[0] // (2 * STEP)
    slot_lane = iota((LANES, LANES), 1)

    def hot_of(ids):
        return (iota((ids.shape[0], rows), 1) == ids).astype(F32).astype(BF16)

    def gather_first(step, to_ref):
        hots = []
        for c in range(STEP // LANES):
            column = step * (STEP // LANES) + c
            hots.append(
                hot_of(jnp.sum(jnp.where(slot_lane == column, slot_ref[...], 0), axis=1, keepdims=True))
            )
        to_ref[...] = dot(jnp.concatenate(hots, axis=0), first_ref[...]).astype(BF16)

    def make_left(step, from_ref):
        for t in range(per_step):
            owner = jnp.clip(owner_ref[0, step * per_step + t], 0, groups - 1)
            stacked = jnp.concatenate(
                [
                    from_ref[t * TILE : (t + 1) * TILE, p * LANES : (p + 1) * LANES]
                    for p in range(D1 // 2)
                ],
                axis=0,
            )
            pair = pair_ref[pl.ds(owner, 1)].reshape(2 * rank, 2 * wide)
            product = dot(stacked, pair)
            for p in range(D1 // 2):
                for half in range(2):
                    for s in range(TILE // 8):
                        spread_ref[t, pl.ds(s * 64 + 2 * p + half, 8, stride=D1), :] = product[
                            p * TILE + s * 8 : p * TILE + s * 8 + 8, half * wide : (half + 1) * wide
                        ]
            left_ref[pl.ds((step * per_step + t) * TILE, TILE)] = (
                spread_ref[t].reshape(TILE, D1, wide).astype(BF16)
            )

    gather_first(0, cores_a_ref)

    def left_pair(pair, carry):
        @pl.when(pair == pairs // 2)
        def _():
            wait(spread_on())
            start(forward([2]))
            wait(forward([1, 3]))
            start(forward_on([1, 3]))

        gather_first(2 * pair + 1, cores_b_ref)
        make_left(2 * pair, cores_a_ref)
        gather_first(2 * pair + 2, cores_a_ref)
        make_left(2 * pair + 1, cores_b_ref)
        return carry

    lax.fori_loop(0, pairs, left_pair, 0)

    group = TILE
    unit = diag_a_ref.shape[0]
    units = mine // unit
    per_unit = unit // group
    id_lane = iota((unit, LANES), 1)
    low_half = iota((group, LANES), 1) < rank
    own = (iota((group, LANES), 1) >> 3) == (iota((group, LANES), 0) & 15)
    def gather_last(source, number, to_ref):
        rows_here = last_ids_ref[number * unit : (number + 1) * unit, :]
        hots = []
        for k in range(BAG):
            mark = source * got_ref.shape[1] + 2 * BAG + k
            ids = jnp.sum(jnp.where(id_lane == mark, rows_here, 0.0), axis=1, keepdims=True)
            hots.append(hot_of(ids.astype(I32)))
        to_ref[...] = dot(jnp.concatenate(hots, axis=0), last_by_d3_ref[...])

    def make_group(source, number, part, from_ref, diag_ref):
        base = number * unit + part * group
        which = number * per_unit + part
        for k in range(BAG):
            for q in range(group):
                at = dest_ref[k * shards + source, base + q]
                staged_ref[which, k, q] = left_ref[at]
        right = jnp.concatenate(
            [staged_ref[which, k].reshape(group * D1, wide) for k in range(BAG)], axis=1
        )
        pieces = [[None] * BAG for _ in range(D2 * D3)]
        for k in range(BAG):
            start = k * unit + part * group
            for tile in range(D3 // 2):
                both = from_ref[start : start + group, tile * LANES : (tile + 1) * LANES]
                low = jnp.where(low_half, both, 0.0)
                high = jnp.where(low_half, 0.0, both)
                pieces[2 * tile][k] = low
                pieces[D3 + 2 * tile][k] = pltpu.roll(low, rank, 1)
                pieces[2 * tile + 1][k] = pltpu.roll(high, rank, 1)
                pieces[D3 + 2 * tile + 1][k] = high
        lasts = jnp.concatenate([jnp.concatenate(p, axis=1) for p in pieces], axis=0).astype(BF16)
        product = dot_nt(lasts, right)
        for e in range(D2 * D3):
            at = e * group
            mine = jnp.concatenate(
                [product[at : at + 16, :LANES], product[at + 16 : at + 32, LANES:]], axis=0
            )
            diag_ref[part * group : (part + 1) * group, e * LANES : (e + 1) * LANES] = jnp.where(
                own, mine, 0.0
            ).astype(BF16)

    def make_unit(to, number, from_ref, diag_ref):
        for part in range(per_unit):
            make_group(to, number, part, from_ref, diag_ref)
        out_ref[to, number * unit : (number + 1) * unit, :] = dot(
            diag_ref[...], gather_own_ref[...]
        ).astype(BF16)

    def send_of(i):
        to = lax.rem(me + 1 + i, shards)
        return pltpu.make_async_remote_copy(
            src_ref=out_ref.at[to],
            dst_ref=recv_ref.at[me],
            send_sem=pooled_send.at[i],
            recv_sem=pooled_recv.at[i],
            device_id={"tables": to},
            device_id_type=MESH,
        )

    gather_last(lax.rem(me + 1, shards), 0, last_a_ref)

    def make_owner(i, carry):
        @pl.when(i == 3)
        def _():
            wait(forward([2]))
            start(forward_on([2]))

        to, after = lax.rem(me + 1 + i, shards), lax.rem(me + 2 + i, shards)
        gather_last(to, 1, last_b_ref)
        make_unit(to, 0, last_a_ref, diag_a_ref)
        gather_last(after, 0, last_a_ref)
        make_unit(to, 1, last_b_ref, diag_b_ref)

        @pl.when(i < shards - 1)
        def _():
            send_of(i).start()

        return carry

    lax.fori_loop(0, shards, make_owner, 0)
    keep.wait()
    wait(forward_on([0, 1, 3, 2]))
    fetches[2].start()
    recv_ref[me] = out_ref[me]
    for i in range(shards - 1):
        send_of(i).wait()
    fetches[0].wait()
    fetches[1].wait()

    first = jnp.concatenate([recv_ref[t] for t in range(shards)], axis=1).astype(F32)
    crossed = first
    for layer in range(down_v.shape[0]):
        low = dot(crossed.astype(BF16), down_v[layer]).astype(BF16)
        lifted = dot(low, up_v[layer])
        crossed = first * (lifted + bias_ref[layer : layer + 1, :].astype(F32)) + crossed
    mine_ref[...] = crossed.astype(BF16)
    pair = pltpu.make_async_remote_copy(
        src_ref=mine_ref, dst_ref=theirs_ref, send_sem=pair_send, recv_sem=pair_recv,
        device_id={"replica": sibling}, device_id_type=MESH,
    )
    pair.start()
    fetches[2].wait()

    def add_units(rows_ref, to_ref, begin, end):
        def step(t, carry):
            weight = jnp.concatenate(
                [left_ref[pl.ds((2 * t + h) * span, span)].reshape(span * D1, lanes) for h in range(2)], axis=1
            )
            hidden = dot(rows_ref[...], weight)
            for h in range(2):
                at = 2 * t + h
                unit = hidden[:, h * lanes : (h + 1) * lanes] + units_ref[pl.ds(2 * at + core, 1), :]
                unit = jnp.maximum(unit, 0.0).astype(BF16).astype(F32)
                to_ref[:mine] += unit * units_ref[pl.ds(2 * (shards + at) + core, 1), :]
            return carry

        lax.fori_loop(begin, end, step, 0)

    def as_row(from_ref):
        return jnp.sum(jnp.transpose(from_ref[...]), axis=0, keepdims=True)

    ours_ref, their_sum_ref = sum_ref.at[0], sum_ref.at[1]
    sum_ref[...] = jnp.zeros_like(sum_ref)
    steps = shards // 2
    add_units(mine_ref, ours_ref, 0, steps // 2)
    pair.wait()
    add_units(theirs_ref, their_sum_ref, 0, steps)
    part_ref[...] = jnp.broadcast_to(as_row(their_sum_ref), part_ref.shape)
    back = pltpu.make_async_remote_copy(
        src_ref=part_ref, dst_ref=part_in_ref, send_sem=part_send, recv_sem=part_recv,
        device_id={"replica": sibling}, device_id_type=MESH,
    )
    back.start()
    add_units(mine_ref, ours_ref, steps // 2, steps)
    ours = as_row(ours_ref)
    back.wait()
    logits = (ours + part_in_ref[:1])[:, :mine] + prior_ref[...]
    both_ref[:1] = logits
    clicks = 1.0 / (1.0 + jnp.exp(-logits))
    click_ref[0] = jnp.broadcast_to(jnp.sum(clicks, axis=1, keepdims=True), click_ref.shape[1:])
    tells = []
    for i in range(1, replicas):
        tells.append(
            pltpu.make_async_remote_copy(
                src_ref=click_ref.at[0],
                dst_ref=click_ref.at[i],
                send_sem=click_send.at[i],
                recv_sem=click_recv.at[i],
                device_id={"replica": lax.rem(rep + i, replicas)},
                device_id_type=MESH,
            )
        )
    for tell in tells:
        tell.start()
    for tell in tells:
        tell.wait()
    total = click_ref[0]
    for i in range(1, replicas):
        total = total + click_ref[i]
    both_ref[1:] = (replicas * mine) * clicks / total[:1, :1]


def main(
    idx_first, idx_middle, idx_last, lengths, core_first, core_middle, core_last,
    top_weight, cross_down, cross_up, cross_bias, units, prior,
):
    groups, rank, wide = core_middle.shape
    shards, replicas = lax.axis_size("tables"), lax.axis_size("replica")
    queries = prior.shape[1]
    items = shards * queries * BAG
    slots = -(-(items + groups * TILE) // (2 * STEP)) * 2 * STEP
    feat, hid = top_weight.shape
    padded = -(-queries // LANES) * LANES
    unit = queries // 2
    owners = -(-(slots // TILE) // LANES) * LANES
    side = 4 if shards == 16 else 1
    vmem = pl.BlockSpec(memory_space=pltpu.VMEM)
    anywhere = pl.BlockSpec(memory_space=pl.ANY)
    dma = pltpu.SemaphoreType.DMA
    return pl.pallas_call(
        main_kernel,
        out_shape=(
            jax.ShapeDtypeStruct((2, queries), F32),
            jax.ShapeDtypeStruct((shards * feat // D1, D1, LANES), BF16),
        ),
        in_specs=[vmem] * 7 + [anywhere] * 3 + [vmem] * 3,
        out_specs=(vmem, anywhere),
        scratch_shapes=[
            pltpu.VMEM((shards, 8, padded), I32),
            pltpu.VMEM((shards, 8, padded), I32),
            pltpu.VMEM((padded, shards * 8), F32),
            pltpu.VMEM((BAG * shards, padded), I32),
            pltpu.VMEM((8, owners), I32),
            pltpu.VMEM((LANES, LANES), I32),
            pltpu.VMEM((BAG * shards, padded), F32),
            pltpu.VMEM((2 * LANES, LANES), F32),
            pltpu.SMEM((BAG * shards, padded), I32),
            pltpu.SMEM((8, owners), I32),
            pltpu.VMEM((groups, 2 * rank, 2 * wide), BF16),
            pltpu.VMEM(core_last.shape, BF16),
            pltpu.VMEM((slots, D1, wide), BF16),
            pltpu.VMEM((STEP // TILE, TILE * D1, wide), F32),
            pltpu.VMEM((STEP, core_first.shape[1]), BF16),
            pltpu.VMEM((STEP, core_first.shape[1]), BF16),
            pltpu.VMEM((BAG * unit, core_last.shape[1]), F32),
            pltpu.VMEM((BAG * unit, core_last.shape[1]), F32),
            pltpu.VMEM((queries // TILE, BAG, TILE, D1, wide), BF16),
            pltpu.VMEM((unit, D2 * D3 * LANES), BF16),
            pltpu.VMEM((unit, D2 * D3 * LANES), BF16),
            pltpu.VMEM((D2 * D3 * LANES, LANES), BF16),
            pltpu.VMEM((shards, queries, LANES), BF16),
            pltpu.VMEM((shards, queries, LANES), BF16),
            pltpu.VMEM((queries, feat), BF16),
            pltpu.VMEM((queries, feat), BF16),
            pltpu.VMEM(cross_down.shape, BF16),
            pltpu.VMEM(cross_up.shape, BF16),
            pltpu.VMEM((8, padded), F32),
            pltpu.VMEM((8, padded), F32),
            pltpu.VMEM((replicas, 8, LANES), F32),
            pltpu.VMEM((2, padded, LANES), F32),
            dma((shards,)),
            dma((shards,)),
            dma((2, 2, 2)),
            dma((2, 2, 2)),
            dma((2, 2, 2, side)),
            dma((2, 2, 2, side)),
            dma,
            dma((shards,)),
            dma((shards,)),
            dma((5,)),
            dma,
            dma,
            dma,
            dma,
            dma((replicas,)),
            dma((replicas,)),
        ],
        compiler_params=pltpu.CompilerParams(
            collective_id=1, has_side_effects=True, vmem_limit_bytes=60 * 2**20
        ),
        cost_estimate=pl.CostEstimate(flops=int(100e9), bytes_accessed=24000000, transcendentals=0),
        name="main",
    )(
        idx_first, idx_middle, idx_last, lengths, core_first, core_middle, core_last,
        top_weight.reshape(feat // D1, D1, hid), cross_down, cross_up, cross_bias, units, prior,
    )


def body(
    core_first,
    core_middle,
    core_last,
    idx_first,
    idx_middle,
    idx_last,
    bag_lengths,
    cross_down,
    cross_up,
    cross_bias,
    top_weight,
    top_bias,
    out_weight,
    prior,
):
    def by_table(values):
        return jnp.transpose(values[0, 0], (1, 2, 0))

    units = jnp.concatenate([top_bias, out_weight]).astype(F32).reshape(-1, LANES)
    both, _ = main(
        by_table(idx_first),
        by_table(idx_middle),
        by_table(idx_last),
        bag_lengths[0, 0].T,
        core_first[0],
        core_middle[0],
        core_last[0],
        top_weight,
        cross_down,
        cross_up,
        cross_bias,
        units,
        prior[0],
    )
    return (both[:1][None], both[1:][None])


def solution(mesh):
    in_specs = (
        P("tables", None, None),
        P("tables", None, None, None),
        P("tables", None, None),
        P("replica", "tables", None, None, None),
        P("replica", "tables", None, None, None),
        P("replica", "tables", None, None, None),
        P("replica", "tables", None, None),
        P(),
        P(),
        P(),
        P(None, "tables"),
        P(),
        P(),
        P("replica", "tables", None),
    )
    out_specs = (P("replica", "tables", None), P("replica", "tables", None))
    return jax.shard_map(body, mesh=mesh, in_specs=in_specs, out_specs=out_specs, check_vma=False)
```

```python
import jax
import jax.numpy as jnp
from jax import lax
from jax.experimental import pallas as pl
from jax.experimental.pallas import tpu as pltpu
from jax.sharding import PartitionSpec as P

D1 = 8
D2 = 2
D3 = 8
BAG = 2
TILE = 32
LANES = 128
STEP = 512

BF16 = jnp.bfloat16
F32 = jnp.float32
I32 = jnp.int32
MESH = pl.DeviceIdType.MESH


def iota(shape, dim):
    return lax.broadcasted_iota(I32, shape, dim)


def dot(a, b):
    return jnp.dot(a, b, preferred_element_type=F32)


def dot_nt(a, b):
    return lax.dot_general(a, b, (((1,), (1,)), ((), ())), preferred_element_type=F32)


def group_items(groups, slots, got_ref, dest_ref, owner_ref, slot_ref, rank_ref, sums_ref):
    sources, _, width = got_ref.shape
    group_row = iota((groups, width), 0)
    lane_row = iota((LANES, width), 0)
    before = (iota((width, width), 0) < iota((width, width), 1)).astype(F32).astype(BF16)
    together = 8
    steps = BAG * sources // together
    per_bag = sources // together

    def rows_of(step, field):
        rows = []
        for u in range(together):
            source = lax.rem(step, per_bag) * together + u
            at = field * BAG + lax.div(step, per_bag)
            rows.append(got_ref[source, pl.ds(at, 1), :])
        return rows

    def count(step, seen):
        hots = [group_row == row for row in rows_of(step, 1)]
        ones = jnp.concatenate([h.astype(F32) for h in hots], axis=0)
        ranks = dot(ones.astype(BF16), before)
        sizes = jnp.sum(ones, axis=1, keepdims=True)
        rows = []
        for u in range(together):
            at = slice(u * groups, (u + 1) * groups)
            rows.append(jnp.sum(jnp.where(hots[u], ranks[at] + seen, 0.0), axis=0, keepdims=True))
            seen = seen + sizes[at]
        rank_ref[pl.ds(pl.multiple_of(step * together, together), together), :] = jnp.concatenate(rows, axis=0)
        return seen

    counts = lax.fori_loop(0, steps, count, jnp.zeros((groups, 1), F32))
    tiles = jnp.floor((counts + (TILE - 1)) * (1.0 / TILE))
    tiles = jnp.broadcast_to(tiles, (groups, LANES))
    high = jnp.floor(tiles * (1.0 / 16))
    low = tiles - 16.0 * high
    above = (iota((groups, groups), 0) > iota((groups, groups), 1)).astype(F32).astype(BF16)
    offset = 16.0 * dot(above, high.astype(BF16)) + dot(above, low.astype(BF16))
    offset = offset[:, :1]
    tile_lane = iota((groups, owner_ref.shape[1]), 1)
    reached = jnp.sum((offset.astype(I32) <= tile_lane).astype(I32), axis=0, keepdims=True)
    owner_ref[...] = jnp.broadcast_to(jnp.clip(reached - 1, 0, groups - 1), owner_ref.shape)
    sums_ref[...] = jnp.zeros_like(sums_ref)

    def place(step, carry):
        first = pl.multiple_of(step * together, together)
        middles = rows_of(step, 1)
        starts = [jnp.sum(jnp.where(group_row == row, offset, 0.0), axis=0, keepdims=True) for row in middles]
        dests = (rank_ref[pl.ds(first, together), :] + TILE * jnp.concatenate(starts, axis=0)).astype(I32)
        dests = jnp.where(jnp.concatenate(middles, axis=0) < 0, -1, dests)
        dest_ref[pl.ds(first, together), :] = jnp.clip(dests, 0, slots - 1)
        ids = jnp.concatenate(rows_of(step, 0), axis=0)
        lanes, highs, lows, rows = dests & (LANES - 1), (ids >> 4).astype(F32), (ids & 15).astype(F32), dests >> 7
        values, spots = [], []
        for u in range(together):
            at = slice(u, u + 1)
            at_lane = lane_row == lanes[at]
            values.append(
                jnp.concatenate(
                    [jnp.where(at_lane, highs[at], 0.0), jnp.where(at_lane, lows[at], 0.0)], axis=0
                ).astype(BF16)
            )
            spots.append((lane_row == rows[at]).astype(F32).astype(BF16))
        sums_ref[...] += dot_nt(jnp.concatenate(values, axis=1), jnp.concatenate(spots, axis=1))
        return carry

    lax.fori_loop(0, steps, place, 0)
    slot_ref[...] = (16.0 * sums_ref[:LANES, :] + sums_ref[LANES:, :]).astype(I32)


def main_kernel(
    idx_first_ref, idx_middle_ref, idx_last_ref, lengths_ref, first_ref, middle_ref, last_ref,
    top_ref, down_ref, up_ref, bias_ref, units_ref, prior_ref,
    both_ref, weight_ref,
    sent_ref, got_ref, last_ids_ref, dest_v, owner_v, slot_ref, rank_ref, places_ref, dest_ref, owner_ref,
    pair_ref, last_by_d3_ref, left_ref, spread_ref, cores_a_ref, cores_b_ref, last_a_ref, last_b_ref,
    staged_ref, diag_a_ref, diag_b_ref, gather_own_ref,
    out_ref, recv_ref, mine_ref, theirs_ref, down_v, up_v, part_ref, part_in_ref, click_ref, sum_ref,
    ids_send, ids_recv, spread_send, spread_recv, forward_send, forward_recv, local_sem,
    pooled_send, pooled_recv, weight_sem, pair_send, pair_recv, part_send, part_recv,
    click_send, click_recv,
):
    shards, mine, lanes = recv_ref.shape
    replicas = lax.axis_size("replica")
    me, rep = lax.axis_index("tables"), lax.axis_index("replica")
    sibling = rep + 1 - 2 * lax.rem(rep, 2)
    barrier = pltpu.get_barrier_semaphore()
    for i in range(1, shards):
        pl.semaphore_signal(
            barrier, inc=1, device_id={"tables": lax.rem(me + i, shards)}, device_id_type=MESH
        )
    for i in range(1, replicas):
        pl.semaphore_signal(
            barrier, inc=1, device_id={"replica": lax.rem(rep + i, replicas)}, device_id_type=MESH
        )
    core = lax.rem(rep, 2)
    groups, rank, wide = middle_ref.shape
    rows = first_ref.shape[0]
    side = 4 if shards == 16 else 1
    row, column = lax.div(me, side), lax.rem(me, side)
    span = down_v.shape[1] // D1
    fetches = [
        pltpu.make_async_copy(down_ref, down_v, weight_sem.at[0]),
        pltpu.make_async_copy(up_ref, up_v, weight_sem.at[1]),
        pltpu.make_async_copy(weight_ref, left_ref.at[pl.ds(0, weight_ref.shape[0])], weight_sem.at[2]),
    ]
    fetches[0].start()
    fetches[1].start()

    rows_of_part = span // 2
    keep = pltpu.make_async_copy(
        top_ref.at[:, :, pl.ds(pl.multiple_of(core * lanes, lanes), lanes)],
        weight_ref.at[pl.ds(me * span, span)],
        local_sem,
    )
    keep.start()

    def place_of(part, along, across):
        u, v = (column, row) if part == 0 else (row, column)
        u, v = lax.rem(u + along + side, side), lax.rem(v + across + side, side)
        return v * side + u if part == 0 else u * side + v

    def hop(part, shard, to, piece, mine_too, sems, at):
        start, count = part * rows_of_part, rows_of_part
        if piece is not None:
            count = rows_of_part // 2
            start = start + piece * count
        dst = weight_ref.at[pl.ds(shard * span + start, count)]
        src = dst
        if mine_too:
            src = top_ref.at[pl.ds(start, count), :, pl.ds(pl.multiple_of(core * lanes, lanes), lanes)]
        return pltpu.make_async_remote_copy(
            src_ref=src, dst_ref=dst, send_sem=sems[0].at[at], recv_sem=sems[1].at[at],
            device_id={"tables": to}, device_id_type=MESH,
        )

    ways = [(part, way, 1 - 2 * way) for part in range(2) for way in range(2)]

    def spread():
        return [
            hop(p, me, place_of(p, d, 0), None, True, (spread_send, spread_recv), (p, w, 0)) for p, w, d in ways
        ]

    def spread_on():
        return [
            hop(p, place_of(p, -d, 0), place_of(p, d, 0), w, False, (spread_send, spread_recv), (p, w, 1))
            for p, w, d in ways
        ]

    def forward(others):
        return [
            hop(
                p, place_of(p, j, 0), place_of(p, 0, d), None, j == 0, (forward_send, forward_recv), (p, w, 0, j)
            )
            for j in others
            for p, w, d in ways
        ]

    def forward_on(others):
        return [
            hop(
                p, place_of(p, j, -d), place_of(p, 0, d), w, False, (forward_send, forward_recv), (p, w, 1, j)
            )
            for j in others
            for p, w, d in ways
        ]

    def start(copies):
        for copy in copies:
            copy.start()

    def wait(copies):
        for copy in copies:
            copy.wait()

    sent_ref[...] = jnp.full_like(sent_ref, -1)
    for t in range(shards):
        in_bag = iota((BAG, mine), 0) < lengths_ref[t : t + 1, :]
        sent_ref[t, 0:BAG, :mine] = idx_first_ref[t]
        sent_ref[t, BAG : 2 * BAG, :mine] = idx_middle_ref[t]
        sent_ref[t, 2 * BAG : 3 * BAG, :mine] = jnp.where(in_bag, idx_last_ref[t], -1)

    def ids_of(i):
        to = lax.rem(me + i, shards)
        return pltpu.make_async_remote_copy(
            src_ref=sent_ref.at[to], dst_ref=got_ref.at[me],
            send_sem=ids_send.at[i], recv_sem=ids_recv.at[i],
            device_id={"tables": to}, device_id_type=MESH,
        )

    pl.semaphore_wait(barrier, shards + replicas - 2)
    for i in range(1, shards):
        ids_of(i).start()
    start(spread())
    start(forward([0]))
    got_ref[me] = sent_ref[me]

    def make_pair(g, carry):
        core = middle_ref[pl.ds(g, 1)].reshape(rank, wide)
        zero = jnp.zeros_like(core)
        pair_ref[pl.ds(g, 1), :rank, :wide] = core.reshape(1, rank, wide)
        pair_ref[pl.ds(g, 1), :rank, wide:] = zero.reshape(1, rank, wide)
        pair_ref[pl.ds(g, 1), rank:, :wide] = zero.reshape(1, rank, wide)
        pair_ref[pl.ds(g, 1), rank:, wide:] = core.reshape(1, rank, wide)
        return carry

    lax.fori_loop(0, groups, make_pair, 0)
    width = last_ref.shape[1]
    from_row, to_lane = iota((width, width), 0), iota((width, width), 1)
    swap = (to_lane == (from_row & (D3 - 1)) * rank + (from_row >> 3)).astype(F32).astype(BF16)
    last_by_d3_ref[...] = dot(last_ref[...], swap).astype(BF16)

    taps = D2 * D3 * LANES
    tap, spot = iota((taps, LANES), 0), iota((taps, LANES), 1)
    gather_own_ref[...] = (spot == (tap & (D1 - 1)) * (D2 * D3) + (tap >> 7)).astype(F32).astype(BF16)

    for i in range(1, shards):
        ids_of(i).wait()
    group_items(groups, left_ref.shape[0], got_ref, dest_v, owner_v, slot_ref, rank_ref, places_ref)
    to_scalars = [
        pltpu.make_async_copy(dest_v, dest_ref, weight_sem.at[3]),
        pltpu.make_async_copy(owner_v, owner_ref, weight_sem.at[4]),
    ]
    for copy in to_scalars:
        copy.start()
    last_ids_ref[...] = jnp.transpose(
        got_ref[...].reshape(shards * got_ref.shape[1], got_ref.shape[2]).astype(F32)
    )
    wait(spread())
    start(spread_on())
    start(forward([1, 3]))
    wait(forward([0]))
    start(forward_on([0]))
    for copy in to_scalars:
        copy.wait()

    per_step = STEP // TILE
    steps_left = left_ref.shape[0] // STEP
    pairs = steps_left // 2
    slot_lane = iota((LANES, LANES), 1)

    def hot_of(ids):
        return (iota((ids.shape[0], rows), 1) == ids).astype(F32).astype(BF16)

    def gather_first(step, to_ref):
        hots = []
        for c in range(STEP // LANES):
            column = step * (STEP // LANES) + c
            hots.append(
                hot_of(jnp.sum(jnp.where(slot_lane == column, slot_ref[...], 0), axis=1, keepdims=True))
            )
        to_ref[...] = dot(jnp.concatenate(hots, axis=0), first_ref[...]).astype(BF16)

    def make_left(step, from_ref):
        for t in range(per_step):
            owner = jnp.clip(owner_ref[0, step * per_step + t], 0, groups - 1)
            stacked = jnp.concatenate(
                [
                    from_ref[t * TILE : (t + 1) * TILE, p * LANES : (p + 1) * LANES]
                    for p in range(D1 // 2)
                ],
                axis=0,
            )
            pair = pair_ref[pl.ds(owner, 1)].reshape(2 * rank, 2 * wide)
            product = dot(stacked, pair)
            for p in range(D1 // 2):
                for half in range(2):
                    for s in range(TILE // 8):
                        spread_ref[t, pl.ds(s * 64 + 2 * p + half, 8, stride=D1), :] = product[
                            p * TILE + s * 8 : p * TILE + s * 8 + 8, half * wide : (half + 1) * wide
                        ]
            left_ref[pl.ds((step * per_step + t) * TILE, TILE)] = (
                spread_ref[t].reshape(TILE, D1, wide).astype(BF16)
            )

    gather_first(0, cores_a_ref)

    def left_pair(pair, carry):
        @pl.when(pair == pairs // 2)
        def _():
            wait(spread_on())
            start(forward([2]))
            wait(forward([1, 3]))
            start(forward_on([1, 3]))

        gather_first(2 * pair + 1, cores_b_ref)
        make_left(2 * pair, cores_a_ref)
        gather_first(2 * pair + 2, cores_a_ref)
        make_left(2 * pair + 1, cores_b_ref)
        return carry

    lax.fori_loop(0, pairs, left_pair, 0)
    if steps_left % 2:
        make_left(steps_left - 1, cores_a_ref)

    group = TILE
    unit = diag_a_ref.shape[0]
    units = mine // unit
    per_unit = unit // group
    id_lane = iota((unit, LANES), 1)
    low_half = iota((group, LANES), 1) < rank
    own = (iota((group, LANES), 1) >> 3) == (iota((group, LANES), 0) & 15)
    def gather_last(source, number, to_ref):
        rows_here = last_ids_ref[number * unit : (number + 1) * unit, :]
        hots = []
        for k in range(BAG):
            mark = source * got_ref.shape[1] + 2 * BAG + k
            ids = jnp.sum(jnp.where(id_lane == mark, rows_here, 0.0), axis=1, keepdims=True)
            hots.append(hot_of(ids.astype(I32)))
        to_ref[...] = dot(jnp.concatenate(hots, axis=0), last_by_d3_ref[...])

    def make_group(source, number, part, from_ref, diag_ref):
        base = number * unit + part * group
        which = number * per_unit + part
        for k in range(BAG):
            for q in range(group):
                at = dest_ref[k * shards + source, base + q]
                staged_ref[which, k, q] = left_ref[at]
        right = jnp.concatenate(
            [staged_ref[which, k].reshape(group * D1, wide) for k in range(BAG)], axis=1
        )
        pieces = [[None] * BAG for _ in range(D2 * D3)]
        for k in range(BAG):
            start = k * unit + part * group
            for tile in range(D3 // 2):
                both = from_ref[start : start + group, tile * LANES : (tile + 1) * LANES]
                low = jnp.where(low_half, both, 0.0)
                high = jnp.where(low_half, 0.0, both)
                pieces[2 * tile][k] = low
                pieces[D3 + 2 * tile][k] = pltpu.roll(low, rank, 1)
                pieces[2 * tile + 1][k] = pltpu.roll(high, rank, 1)
                pieces[D3 + 2 * tile + 1][k] = high
        lasts = jnp.concatenate([jnp.concatenate(p, axis=1) for p in pieces], axis=0).astype(BF16)
        product = dot_nt(lasts, right)
        for e in range(D2 * D3):
            at = e * group
            mine = jnp.concatenate(
                [product[at : at + 16, :LANES], product[at + 16 : at + 32, LANES:]], axis=0
            )
            diag_ref[part * group : (part + 1) * group, e * LANES : (e + 1) * LANES] = jnp.where(
                own, mine, 0.0
            ).astype(BF16)

    def make_unit(to, number, from_ref, diag_ref):
        for part in range(per_unit):
            make_group(to, number, part, from_ref, diag_ref)
        out_ref[to, number * unit : (number + 1) * unit, :] = dot(
            diag_ref[...], gather_own_ref[...]
        ).astype(BF16)

    def send_of(i):
        to = lax.rem(me + 1 + i, shards)
        return pltpu.make_async_remote_copy(
            src_ref=out_ref.at[to],
            dst_ref=recv_ref.at[me],
            send_sem=pooled_send.at[i],
            recv_sem=pooled_recv.at[i],
            device_id={"tables": to},
            device_id_type=MESH,
        )

    gather_last(lax.rem(me + 1, shards), 0, last_a_ref)

    def make_owner(i, carry):
        @pl.when(i == 3)
        def _():
            wait(forward([2]))
            start(forward_on([2]))

        to, after = lax.rem(me + 1 + i, shards), lax.rem(me + 2 + i, shards)
        gather_last(to, 1, last_b_ref)
        make_unit(to, 0, last_a_ref, diag_a_ref)
        gather_last(after, 0, last_a_ref)
        make_unit(to, 1, last_b_ref, diag_b_ref)

        @pl.when(i < shards - 1)
        def _():
            send_of(i).start()

        return carry

    lax.fori_loop(0, shards, make_owner, 0)
    keep.wait()
    wait(forward_on([0, 1, 3, 2]))
    fetches[2].start()
    recv_ref[me] = out_ref[me]
    for i in range(shards - 1):
        send_of(i).wait()
    fetches[0].wait()
    fetches[1].wait()

    first = jnp.concatenate([recv_ref[t] for t in range(shards)], axis=1).astype(F32)
    crossed = first
    for layer in range(down_v.shape[0]):
        low = dot(crossed.astype(BF16), down_v[layer]).astype(BF16)
        lifted = dot(low, up_v[layer])
        crossed = first * (lifted + bias_ref[layer : layer + 1, :].astype(F32)) + crossed
    mine_ref[...] = crossed.astype(BF16)
    pair = pltpu.make_async_remote_copy(
        src_ref=mine_ref, dst_ref=theirs_ref, send_sem=pair_send, recv_sem=pair_recv,
        device_id={"replica": sibling}, device_id_type=MESH,
    )
    pair.start()
    fetches[2].wait()

    def add_units(rows_ref, to_ref, begin, end):
        def step(t, carry):
            weight = jnp.concatenate(
                [left_ref[pl.ds((2 * t + h) * span, span)].reshape(span * D1, lanes) for h in range(2)], axis=1
            )
            hidden = dot(rows_ref[...], weight)
            for h in range(2):
                at = 2 * t + h
                unit = hidden[:, h * lanes : (h + 1) * lanes] + units_ref[pl.ds(2 * at + core, 1), :]
                unit = jnp.maximum(unit, 0.0).astype(BF16).astype(F32)
                to_ref[:mine] += unit * units_ref[pl.ds(2 * (shards + at) + core, 1), :]
            return carry

        lax.fori_loop(begin, end, step, 0)

    def as_row(from_ref):
        return jnp.sum(jnp.transpose(from_ref[...]), axis=0, keepdims=True)

    ours_ref, their_sum_ref = sum_ref.at[0], sum_ref.at[1]
    sum_ref[...] = jnp.zeros_like(sum_ref)
    steps = shards // 2
    add_units(mine_ref, ours_ref, 0, steps // 2)
    pair.wait()
    add_units(theirs_ref, their_sum_ref, 0, steps)
    part_ref[...] = jnp.broadcast_to(as_row(their_sum_ref), part_ref.shape)
    back = pltpu.make_async_remote_copy(
        src_ref=part_ref, dst_ref=part_in_ref, send_sem=part_send, recv_sem=part_recv,
        device_id={"replica": sibling}, device_id_type=MESH,
    )
    back.start()
    add_units(mine_ref, ours_ref, steps // 2, steps)
    ours = as_row(ours_ref)
    back.wait()
    logits = (ours + part_in_ref[:1])[:, :mine] + prior_ref[...]
    both_ref[:1] = logits
    clicks = 1.0 / (1.0 + jnp.exp(-logits))
    click_ref[0] = jnp.broadcast_to(jnp.sum(clicks, axis=1, keepdims=True), click_ref.shape[1:])
    tells = []
    for i in range(1, replicas):
        tells.append(
            pltpu.make_async_remote_copy(
                src_ref=click_ref.at[0],
                dst_ref=click_ref.at[i],
                send_sem=click_send.at[i],
                recv_sem=click_recv.at[i],
                device_id={"replica": lax.rem(rep + i, replicas)},
                device_id_type=MESH,
            )
        )
    for tell in tells:
        tell.start()
    for tell in tells:
        tell.wait()
    total = click_ref[0]
    for i in range(1, replicas):
        total = total + click_ref[i]
    both_ref[1:] = (replicas * mine) * clicks / total[:1, :1]


def main(
    idx_first, idx_middle, idx_last, lengths, core_first, core_middle, core_last,
    top_weight, cross_down, cross_up, cross_bias, units, prior,
):
    groups, rank, wide = core_middle.shape
    shards, replicas = lax.axis_size("tables"), lax.axis_size("replica")
    queries = prior.shape[1]
    items = shards * queries * BAG
    slots = -(-(items + groups * TILE) // STEP) * STEP
    feat, hid = top_weight.shape
    padded = -(-queries // LANES) * LANES
    unit = queries // 2
    owners = -(-(slots // TILE) // LANES) * LANES
    side = 4 if shards == 16 else 1
    vmem = pl.BlockSpec(memory_space=pltpu.VMEM)
    anywhere = pl.BlockSpec(memory_space=pl.ANY)
    dma = pltpu.SemaphoreType.DMA
    return pl.pallas_call(
        main_kernel,
        out_shape=(
            jax.ShapeDtypeStruct((2, queries), F32),
            jax.ShapeDtypeStruct((shards * feat // D1, D1, LANES), BF16),
        ),
        in_specs=[vmem] * 7 + [anywhere] * 3 + [vmem] * 3,
        out_specs=(vmem, anywhere),
        scratch_shapes=[
            pltpu.VMEM((shards, 8, padded), I32),
            pltpu.VMEM((shards, 8, padded), I32),
            pltpu.VMEM((padded, shards * 8), F32),
            pltpu.VMEM((BAG * shards, padded), I32),
            pltpu.VMEM((8, owners), I32),
            pltpu.VMEM((LANES, LANES), I32),
            pltpu.VMEM((BAG * shards, padded), F32),
            pltpu.VMEM((2 * LANES, LANES), F32),
            pltpu.SMEM((BAG * shards, padded), I32),
            pltpu.SMEM((8, owners), I32),
            pltpu.VMEM((groups, 2 * rank, 2 * wide), BF16),
            pltpu.VMEM(core_last.shape, BF16),
            pltpu.VMEM((slots, D1, wide), BF16),
            pltpu.VMEM((STEP // TILE, TILE * D1, wide), F32),
            pltpu.VMEM((STEP, core_first.shape[1]), BF16),
            pltpu.VMEM((STEP, core_first.shape[1]), BF16),
            pltpu.VMEM((BAG * unit, core_last.shape[1]), F32),
            pltpu.VMEM((BAG * unit, core_last.shape[1]), F32),
            pltpu.VMEM((queries // TILE, BAG, TILE, D1, wide), BF16),
            pltpu.VMEM((unit, D2 * D3 * LANES), BF16),
            pltpu.VMEM((unit, D2 * D3 * LANES), BF16),
            pltpu.VMEM((D2 * D3 * LANES, LANES), BF16),
            pltpu.VMEM((shards, queries, LANES), BF16),
            pltpu.VMEM((shards, queries, LANES), BF16),
            pltpu.VMEM((queries, feat), BF16),
            pltpu.VMEM((queries, feat), BF16),
            pltpu.VMEM(cross_down.shape, BF16),
            pltpu.VMEM(cross_up.shape, BF16),
            pltpu.VMEM((8, padded), F32),
            pltpu.VMEM((8, padded), F32),
            pltpu.VMEM((replicas, 8, LANES), F32),
            pltpu.VMEM((2, padded, LANES), F32),
            dma((shards,)),
            dma((shards,)),
            dma((2, 2, 2)),
            dma((2, 2, 2)),
            dma((2, 2, 2, side)),
            dma((2, 2, 2, side)),
            dma,
            dma((shards,)),
            dma((shards,)),
            dma((5,)),
            dma,
            dma,
            dma,
            dma,
            dma((replicas,)),
            dma((replicas,)),
        ],
        compiler_params=pltpu.CompilerParams(
            collective_id=1, has_side_effects=True, vmem_limit_bytes=60 * 2**20
        ),
        cost_estimate=pl.CostEstimate(flops=int(100e9), bytes_accessed=24000000, transcendentals=0),
        name="main",
    )(
        idx_first, idx_middle, idx_last, lengths, core_first, core_middle, core_last,
        top_weight.reshape(feat // D1, D1, hid), cross_down, cross_up, cross_bias, units, prior,
    )


def body(
    core_first,
    core_middle,
    core_last,
    idx_first,
    idx_middle,
    idx_last,
    bag_lengths,
    cross_down,
    cross_up,
    cross_bias,
    top_weight,
    top_bias,
    out_weight,
    prior,
):
    def by_table(values):
        return jnp.transpose(values[0, 0], (1, 2, 0))

    units = jnp.concatenate([top_bias, out_weight]).astype(F32).reshape(-1, LANES)
    both, _ = main(
        by_table(idx_first),
        by_table(idx_middle),
        by_table(idx_last),
        bag_lengths[0, 0].T,
        core_first[0],
        core_middle[0],
        core_last[0],
        top_weight,
        cross_down,
        cross_up,
        cross_bias,
        units,
        prior[0],
    )
    return (both[:1][None], both[1:][None])


def solution(mesh):
    in_specs = (
        P("tables", None, None),
        P("tables", None, None, None),
        P("tables", None, None),
        P("replica", "tables", None, None, None),
        P("replica", "tables", None, None, None),
        P("replica", "tables", None, None, None),
        P("replica", "tables", None, None),
        P(),
        P(),
        P(),
        P(None, "tables"),
        P(),
        P(),
        P("replica", "tables", None),
    )
    out_specs = (P("replica", "tables", None), P("replica", "tables", None))
    return jax.shard_map(body, mesh=mesh, in_specs=in_specs, out_specs=out_specs, check_vma=False)
```
